128 devices in a mesh: gx: 16 (over z, y), gy: 8 (over x, core).
Axes of the slice: x: 4, y: 4, z: 4, core: 2. Of those that a mesh axis runs over, the one named last changes fastest.
Arguments:
- pressure: float32 [128, 1024, 128], P('gx', 'gy'), may hold values from 0.5 to 1.5
- water_sat: float32 [128, 1024, 128], P('gx', 'gy'), may hold values from 0.1 to 0.45
- gas_sat: float32 [128, 1024, 128], P('gx', 'gy'), may hold values from 0 to 0.4
- mass_old: float32 [3, 128, 1024, 128], P(None, 'gx', 'gy'), may hold values from 0.1 to 0.7
- pore_volume: float32 [128, 1024, 128], P('gx', 'gy'), may hold values from 0.5 to 2
- permeability: float32 [128, 1024, 128], P('gx', 'gy'), may hold values from 0.1 to 10
- newton_scale: float32 [3, 128, 1024, 128], P(None, 'gx', 'gy'), may hold values from 0.1 to 0.4
- conn_factor: float32 [49152, 128], P(('gx', 'gy')), may hold values from 0.2 to 2
- perf_column: int32 [49152], P(('gx', 'gy')), may hold values from 0 to 1023
- perf_owner: int32 [49152, 1], P(('gx', 'gy')), may hold values from 0 to 127; in each aligned block of 384 rows (0 to 383, 384 to 767, ...) at most 6 rows name the same one
- perf_well: int32 [49152], P(('gx', 'gy')), may hold values from 0 to 7
- perf_segment: int32 [49152], P(('gx', 'gy')), may hold values from 0 to 7
- seg_parent: int32 [1024, 8], P(('gx', 'gy')), may hold values from 0 to 6, as said below
- seg_drop: float32 [1024, 8], P(('gx', 'gy')), may hold values from 0.1 to 0.5
- bottom_press: float32 [1024], P(('gx', 'gy')), may hold values from 0.2 to 0.6
Outputs:
- residual: float32 [3, 128, 1024, 128], P(None, 'gx', 'gy')
- seg_pressure: float32 [1024, 8], P(('gx', 'gy'))
The draws below stay inside these ranges and needn't reach their ends.
Inputs may be any that keep to these rules, and one draw needn't show every extreme that they name: `perf_owner`: in the rows of one device at most 6 name the same owner, a bound that some block reaches; every device owns wells with perforations. `seg_parent`: segment 0 of a well is its own parent; the parent of a segment s >= 1 is a segment below s.
All inputs are finite; a program needn't handle non-finite values.
Results may differ from the reference program's by a relative error of at most 0.0003.
Values sent between devices are 32-bit elements; how exact they have to be, the bound alone decides.
A program may use at most 128 MiB of HBM per device.

```python
import math
import jax
import jax.numpy as jnp
import numpy as np
from jax import lax

CX = 8
CY = 128
NZ = 128
P_DEV = 384
WELL_DEV = 8
SEG = 8
CAP = 6
NX = 128
NY = 1024
PERFS = 49152
W = 1024
N_GX = 16
N_GY = 8


def draw_seg_parent(key, part):
    key = jax.random.fold_in(key, 11)
    limit = jnp.maximum(lax.broadcasted_iota(jnp.int32, (W, SEG), 1), 1)
    return jax.random.randint(key, (W, SEG), 0, limit, dtype=jnp.int32)


def place_ends(values, key, smallest, high):
    longest = values.shape.index(max(values.shape))
    spots = []
    for shift in (0, 1):
        where = [jax.random.randint(jax.random.fold_in(key, axis), (), 0, length) for axis, length in enumerate(values.shape)]
        where[longest] = (where[longest] + shift) % values.shape[longest]
        spots.append(tuple(where))
    return values.at[spots[0]].set(smallest).at[spots[1]].set(high)


def steps_of(stream_key, shape, shards, smallest, largest):
    loudness = 1.0
    for axis_at, parts in shards:
        draws = jax.random.uniform(jax.random.fold_in(jax.random.fold_in(stream_key, 6), axis_at), (parts,), jnp.float32, smallest / len(shards), largest / len(shards))
        loudness = loudness * jnp.repeat(jnp.exp(draws), shape[axis_at] // parts).reshape((-1,) + (1,) * (len(shape) - 1 - axis_at))
    return loudness


def shared_out(own_key, own, number, rows, amount, top, most, skew):
    sequence = jax.random.permutation(own_key, amount)
    crowded, ordinary = portions_of(amount, rows * top, most, skew, True), portions_of(amount, rows * top, most, skew, False)
    places = jnp.arange(amount)

    def named(tallies, offset_by):
        used = int((tallies > 0).sum())
        fixed = max(1, used // 4)
        passed = fixed + (places - fixed + offset_by * (used - fixed)) % max(1, amount - fixed)
        return jnp.zeros((amount,), jnp.int32).at[sequence[jnp.where(places < fixed, places, passed)]].set(jnp.asarray(tallies, jnp.int32))

    tallies = jnp.where(number % 4 == 0, named(crowded, number // 4), named(ordinary, number - number // 4 - 1))
    mixed = jax.random.permutation(jax.random.fold_in(own, 3), amount)
    donor, sink = mixed[0:amount // 2 * 2:2], mixed[1:amount // 2 * 2:2]
    room = jnp.minimum(tallies[donor] - 1, most - tallies[sink]) // 2
    room = jnp.where((donor == sequence[0]) | (sink == sequence[0]) | (tallies[sink] == 0), 0, jnp.maximum(room, 0))
    passed = jax.random.randint(jax.random.fold_in(own, 4), (amount // 2,), 0, 1 << 20) % (room + 1)
    tallies = tallies.at[donor].add(-passed).at[sink].add(passed)
    members = jnp.searchsorted(jnp.cumsum(tallies), jnp.arange(rows * top), side="right").astype(jnp.int32)
    table = members.reshape(top, rows).T
    table = table[jax.random.permutation(jax.random.fold_in(own, 1), rows)]
    offset_by = jax.random.randint(jax.random.fold_in(own, 2), (rows, 1), 0, top)
    return jnp.take_along_axis(table, (jnp.arange(top)[None, :] + offset_by) % top, axis=1)


def portions_of(number_of, total, reach, slope, full):
    weights = [(1 << 20) // math.isqrt(standing ** slope) + 1 for standing in range(1, number_of + 1)]
    largest = reach if full else min(reach, max(-(-total // number_of), total * weights[0] // sum(weights)))
    least = 1 if total - largest >= number_of - 1 else 0
    holding, spare = [largest] + [least] * (number_of - 1), total - largest - least * (number_of - 1)
    while spare > 0:
        free = [i for i in range(1, number_of) if holding[i] < largest] or [i for i in range(1, number_of) if holding[i] < reach]
        whole, budget = sum([weights[i] for i in free]), spare
        for i in free:
            addition = min(reach - holding[i], max(1, budget * weights[i] // whole), spare)
            holding[i] = holding[i] + addition
            spare = spare - addition
    return np.array(holding)


def setup_inputs(seed: int = 0) -> dict:
    key_of = jax.random.split(jax.random.key(seed), 16)
    pressure = jnp.clip(0.5 + 1.0 * jax.random.uniform(key_of[0], (NX, NY, NZ), jnp.float32) ** steps_of(key_of[0], (NX, NY, NZ), ((0, 16), (1, 8)), -0.2, 0.2), 0.5, 1.5)
    water_sat = jnp.clip(0.1 + 0.35 * jax.random.uniform(key_of[1], (NX, NY, NZ), jnp.float32) ** steps_of(key_of[1], (NX, NY, NZ), ((0, 16), (1, 8)), -0.2, 0.2), 0.1, 0.45)
    gas_sat = jnp.clip(0.4 * jax.random.uniform(key_of[2], (NX, NY, NZ), jnp.float32) ** steps_of(key_of[2], (NX, NY, NZ), ((0, 16), (1, 8)), -0.2, 0.2), 0.0, 0.4)
    mass_old = jnp.clip(0.1 + 0.59999999 * jax.random.uniform(key_of[3], (3, NX, NY, NZ), jnp.float32) ** steps_of(key_of[3], (3, NX, NY, NZ), ((1, 16), (2, 8)), -0.2, 0.2), 0.1, 0.7)
    pore_volume = jnp.clip(jnp.exp(math.log(2.0) - 1.3862944 * jax.random.uniform(key_of[4], (NX, NY, NZ), jnp.float32) ** steps_of(key_of[4], (NX, NY, NZ), ((0, 16), (1, 8)), -0.2, 0.2)), 0.5, 2.0)
    permeability = jnp.clip(jnp.exp(math.log(10.0) - 4.6051702 * jax.random.uniform(key_of[5], (NX, NY, NZ), jnp.float32) ** steps_of(key_of[5], (NX, NY, NZ), ((0, 16), (1, 8)), -0.2, 0.2)), 0.1, 10.0)
    newton_scale = jnp.clip(jnp.exp(math.log(0.4) - 1.3862944 * jax.random.uniform(key_of[6], (3, NX, NY, NZ), jnp.float32) ** steps_of(key_of[6], (3, NX, NY, NZ), ((1, 16), (2, 8)), -0.2, 0.2)), 0.1, 0.4)
    conn_factor = jnp.clip(jnp.exp(math.log(2.0) - 2.3025851 * jax.random.uniform(key_of[7], (PERFS, NZ), jnp.float32) ** steps_of(key_of[7], (PERFS, NZ), ((0, 128),), -0.2, 0.2)), 0.2, 2.0)
    perf_column = place_ends(jax.random.randint(key_of[8], (PERFS,), 0, CX * CY), jax.random.fold_in(key_of[8], 1), 0, (CX * CY) - 1).astype(jnp.int32)
    perf_owner_keys = jax.random.split(jax.random.fold_in(key_of[9], 1), PERFS // P_DEV)
    perf_owner_turns = jax.random.permutation(jax.random.fold_in(key_of[9], 3), PERFS // P_DEV)
    perf_owner = jax.vmap(lambda own, number: shared_out(jax.random.fold_in(key_of[9], 2), own, number, P_DEV, N_GX * N_GY, 1, CAP, 2))(perf_owner_keys, perf_owner_turns).reshape((PERFS, 1))
    perf_well = place_ends(jax.random.randint(key_of[10], (PERFS,), 0, WELL_DEV), jax.random.fold_in(key_of[10], 1), 0, WELL_DEV - 1).astype(jnp.int32)
    perf_segment = place_ends(jax.random.randint(key_of[11], (PERFS,), 0, SEG), jax.random.fold_in(key_of[11], 1), 0, SEG - 1).astype(jnp.int32)
    seg_parent = draw_seg_parent(jax.random.fold_in(key_of[15], 71), 0)
    seg_drop = jnp.clip(jnp.exp(math.log(0.5) - 1.609438 * jax.random.uniform(key_of[13], (W, SEG), jnp.float32) ** steps_of(key_of[13], (W, SEG), ((0, 128),), -0.2, 0.2)), 0.1, 0.5)
    bottom_press = jnp.clip(0.2 + 0.400000021 * jax.random.uniform(key_of[14], (W,), jnp.float32) ** steps_of(key_of[14], (W,), ((0, 128),), -0.2, 0.2), 0.2, 0.6)
    return dict(pressure=pressure, water_sat=water_sat, gas_sat=gas_sat, mass_old=mass_old, pore_volume=pore_volume, permeability=permeability, newton_scale=newton_scale, conn_factor=conn_factor, perf_column=perf_column, perf_owner=perf_owner, perf_well=perf_well, perf_segment=perf_segment, seg_parent=seg_parent, seg_drop=seg_drop, bottom_press=bottom_press)


MU_OIL = 2.0
MU_WATER = 0.5
MU_GAS = 0.2
RHO_OIL = 0.8
RHO_WATER = 1.0
RHO_GAS = 0.15
RS_COEF = 0.2
KZ_RATIO = 0.1
GRAV_Z = 0.05
GRAV_SEG = 1.0
GRAV_WELL = 0.5
RHO_REF = 0.5


def cell_terms(state):
    pressure_cell = state[0]
    sat_water = state[1]
    sat_gas = state[2]
    sat_oil = 1.0 - sat_water - sat_gas
    b_oil = 1.0 + 0.05 * (pressure_cell - 1.0)
    b_water = 1.0 + 0.02 * (pressure_cell - 1.0)
    b_gas = 0.2 + 0.8 * pressure_cell
    lam_oil = sat_oil * sat_oil / MU_OIL
    lam_water = sat_water * sat_water / MU_WATER
    lam_gas = sat_gas * sat_gas / MU_GAS
    solution = RS_COEF * pressure_cell
    mobility = jnp.stack([lam_oil * b_oil, lam_water * b_water, lam_gas * b_gas, lam_oil * b_oil * solution])
    density = jnp.stack([RHO_OIL * b_oil, RHO_WATER * b_water, RHO_GAS * b_gas])
    lam_total = lam_oil + lam_water + lam_gas
    mix_mass = lam_oil * density[0] + lam_water * density[1] + lam_gas * density[2]
    stored = jnp.stack([b_oil * sat_oil, b_water * sat_water, b_gas * sat_gas + solution * b_oil * sat_oil])
    return pressure_cell, mobility, density, lam_total, mix_mass, stored


def face_flux(first_side, second_side, trans, gravity_head):
    press_one, mobile_one, dense_one = first_side
    press_two, mobile_two, dense_two = second_side
    potential = (press_one - press_two)[None] + gravity_head * 0.5 * (dense_one + dense_two)
    upwind = jnp.where(potential > 0.0, mobile_one[:3], mobile_two[:3])
    flows = trans[None] * upwind * potential
    carried = trans * jnp.where(potential[0] > 0.0, mobile_one[3], mobile_two[3]) * potential[0]
    return jnp.stack([flows[0], flows[1], flows[2] + carried])


def divergence(padded_state, padded_perm):
    full_state = jnp.pad(padded_state, ((0, 0), (0, 0), (0, 0), (1, 1)))
    full_perm = jnp.pad(padded_perm, ((0, 0), (0, 0), (1, 1)))
    pressure_cell, mobility, density, lam_total, mix_mass, stored = cell_terms(full_state)
    outflow = None
    for direction, factor, gravity_head in ((0, 1.0, 0.0), (1, 1.0, 0.0), (2, KZ_RATIO, GRAV_Z)):
        low_index = [slice(1, -1), slice(1, -1), slice(1, -1)]
        high_index = [slice(1, -1), slice(1, -1), slice(1, -1)]
        low_index[direction] = slice(0, -1)
        high_index[direction] = slice(1, None)
        low_cut = tuple(low_index)
        high_cut = tuple(high_index)
        lead_low = (slice(None),) + low_cut
        lead_high = (slice(None),) + high_cut
        perm_low = full_perm[low_cut]
        perm_high = full_perm[high_cut]
        trans = factor * 2.0 * perm_low * perm_high / (perm_low + perm_high)
        flux = face_flux((pressure_cell[low_cut], mobility[lead_low], density[lead_low]),
                         (pressure_cell[high_cut], mobility[lead_high], density[lead_high]), trans, gravity_head)
        faces = flux.shape[direction + 1]
        change = lax.slice_in_dim(flux, 1, faces, axis=direction + 1) - lax.slice_in_dim(flux, 0, faces - 1, axis=direction + 1)
        outflow = change if outflow is None else outflow + change
    inner = (slice(None), slice(1, -1), slice(1, -1), slice(1, -1))
    return outflow, stored[inner]


def column_terms(state, column):
    flat_state = state.reshape(3, state.shape[1] * state.shape[2], state.shape[3])
    return cell_terms(jnp.take(flat_state, column, axis=1))


def segment_pressure(seg_sums, parent, drop, bottom):
    mix_dens = (seg_sums[0] + RHO_REF) / (seg_sums[1] + 1.0)
    rise = GRAV_SEG * mix_dens * drop
    is_root = lax.broadcasted_iota(jnp.int32, drop.shape, 1) == 0
    seg_press = jnp.zeros_like(drop)
    for sweep_index in range(drop.shape[1]):
        seg_press = jnp.where(is_root, bottom[:, None] + rise, jnp.take_along_axis(seg_press, parent, axis=1) + rise)
    return seg_press, mix_dens


def well_rates(terms, conn, seg_press, mix_dens):
    pressure_cell = terms[0]
    mobility = terms[1]
    layers = conn.shape[1]
    depth = (jnp.arange(layers, dtype=jnp.float32) + 0.5) / layers - 0.5
    level = seg_press[:, None] + GRAV_WELL * mix_dens[:, None] * depth[None]
    drive = conn * (pressure_cell - level)
    return jnp.stack([drive * mobility[0], drive * mobility[1], drive * (mobility[2] + mobility[3])])


def spread_rates(rates, column, columns, shape):
    summed = jax.ops.segment_sum(jnp.moveaxis(rates, 0, 1), column, num_segments=columns)
    return jnp.moveaxis(summed, 1, 0).reshape(shape)


def base_residual(state, mass_old, pore_volume, padded_perm):
    padded = jnp.pad(state, ((0, 0), (1, 1), (1, 1), (0, 0)))

    def slab(block_index):
        start = block_index * CX
        part_state = lax.dynamic_slice_in_dim(padded, start, CX + 2, 1)
        part_perm = lax.dynamic_slice_in_dim(padded_perm, start, CX + 2, 0)
        outflow, stored = divergence(part_state, part_perm)
        volume = lax.dynamic_slice_in_dim(pore_volume, start, CX, 0)
        old_part = lax.dynamic_slice_in_dim(mass_old, start, CX, 1)
        return volume[None] * stored - old_part + outflow

    blocks = lax.map(slab, jnp.arange(N_GX, dtype=jnp.int32))
    return jnp.moveaxis(blocks, 0, 1).reshape(3, NX, NY, NZ)


def newton_pass(state, mass_old, pore_volume, padded_perm, conn_factor, global_col, seg_key, seg_parent, seg_drop, bottom_press):
    base = base_residual(state, mass_old, pore_volume, padded_perm)
    terms = column_terms(state, global_col)
    conn_rows = jnp.stack([conn_factor * terms[4], conn_factor * terms[3]], axis=1)
    totals = jnp.sum(conn_rows, axis=2)
    seg_sums = jax.ops.segment_sum(totals, seg_key, num_segments=W * SEG)
    seg_sums = seg_sums.T.reshape(2, W, SEG)
    seg_press, mix_dens = segment_pressure(seg_sums, seg_parent, seg_drop, bottom_press)
    press_along = jnp.take(seg_press.reshape(W * SEG), seg_key)
    dens_along = jnp.take(mix_dens.reshape(W * SEG), seg_key)
    rates = well_rates(terms, conn_factor, press_along, dens_along)
    return base + spread_rates(rates, global_col, NX * NY, base.shape), seg_press


def reference(pressure, water_sat, gas_sat, mass_old, pore_volume, permeability, newton_scale, conn_factor, perf_column, perf_owner, perf_well, perf_segment, seg_parent, seg_drop, bottom_press):
    state = jnp.stack([pressure, water_sat, gas_sat])
    padded_perm = jnp.pad(permeability, ((1, 1), (1, 1), (0, 0)))
    device_of = jnp.arange(PERFS, dtype=jnp.int32) // P_DEV
    column_x = (device_of // N_GY) * CX + perf_column // CY
    column_y = (device_of % N_GY) * CY + perf_column % CY
    global_col = (column_x * NY + column_y).astype(jnp.int32)
    seg_key = ((perf_owner[:, 0] * WELL_DEV + perf_well) * SEG + perf_segment).astype(jnp.int32)
    first, unused = newton_pass(state, mass_old, pore_volume, padded_perm, conn_factor, global_col, seg_key, seg_parent, seg_drop, bottom_press)
    state = state - newton_scale * first
    second, seg_press = newton_pass(state, mass_old, pore_volume, padded_perm, conn_factor, global_col, seg_key, seg_parent, seg_drop, bottom_press)
    return second, seg_press
```

```python
import functools

import jax
import jax.numpy as jnp
from jax import lax
from jax.experimental import pallas as pl
from jax.experimental.pallas import tpu as pltpu
from jax.sharding import PartitionSpec as P

MESH = pl.DeviceIdType.MESH
F32 = jnp.float32
BF16 = jnp.bfloat16
NGX, NGY = 16, 8
CX, CY, NZ = 8, 128, 128
PD = 384
COLS = CX * CY
YB = 32


def split(v):
    hi = v.astype(BF16)
    return hi, (v - hi.astype(F32)).astype(BF16)


def dot2(one_hot, v):
    hi, lo = split(v)
    return jnp.dot(one_hot, hi, preferred_element_type=F32) + jnp.dot(
        one_hot, lo, preferred_element_type=F32
    )


def exact_dot(a, b, dims=(((1,), (0,)), ((), ()))):
    return lax.dot_general(a, b, dims, precision=lax.Precision.HIGHEST, preferred_element_type=F32)


def mobilities(p, sw, sg):
    so = 1.0 - sw - sg
    m1 = (0.5 * so * so) * (0.95 + 0.05 * p)
    m2 = (2.0 * sw * sw) * (0.98 + 0.02 * p)
    m3 = (5.0 * sg * sg) * (0.2 + 0.8 * p)
    m4 = m1 * (0.2 * p)
    return m1, m2, m3, m4


def total_mobility(sw, sg):
    so = 1.0 - sw - sg
    return 0.5 * so * so + 2.0 * sw * sw + 5.0 * sg * sg


def side_flux(p_i, m_i, p_j, m_j, trans):
    d = p_i - p_j
    up = d > 0.0
    t = trans * d
    return [t * jnp.where(up, a, b) for a, b in zip(m_i, m_j)]


def harmonic(a, b):
    return 2.0 * a * b / (a + b)


def kernel(
    p_h, sw_h, sg_h, mo_h, pv_h, k_h, ns_h, cf_h,
    col_ref, own_ref, well_ref, seg_ref, par_ref, drop_ref, bot_ref,
    out_ref, press_ref,
    st1, st2, cf, pv, mo, ns, hx1, hx2, hy1, hy2, hys1, hys2,
    q, tx, ty, tz, txb, tyb, fx, fy, base, c0, wl,
    g, s, a_t, r, lm, mlh, mll,
    tb, r1, x1, r2, x3, r3, w0, wr,
    load_sem, halo_send, halo_recv, ph_send, ph_recv, w_send, w_recv,
):
    gx = lax.axis_index("gx")
    gy = lax.axis_index("gy")

    barrier = pltpu.get_barrier_semaphore()
    for k in range(1, NGX):
        pl.semaphore_signal(barrier, 1, device_id=(lax.rem(gx + k, NGX), gy), device_id_type=MESH)
    for k in range(1, NGY):
        pl.semaphore_signal(barrier, 1, device_id=(gx, lax.rem(gy + k, NGY)), device_id_type=MESH)

    loads = [
        pltpu.make_async_copy(p_h, st1.at[0], load_sem.at[0]),
        pltpu.make_async_copy(sw_h, st1.at[1], load_sem.at[1]),
        pltpu.make_async_copy(sg_h, st1.at[2], load_sem.at[2]),
        pltpu.make_async_copy(cf_h, cf, load_sem.at[3]),
        pltpu.make_async_copy(k_h, st1.at[3], load_sem.at[4]),
        pltpu.make_async_copy(pv_h, pv, load_sem.at[5]),
        pltpu.make_async_copy(mo_h, mo, load_sem.at[6]),
        pltpu.make_async_copy(ns_h, ns, load_sem.at[7]),
    ]
    for load in loads:
        load.start()

    col = col_ref[...]
    own = own_ref[...]
    row = lax.rem(own, NGY) * 8 + seg_ref[...]
    lane = (own // NGY) * 8 + well_ref[...]
    packed = (col + 1024 * row + 65536 * lane).astype(F32)
    packed_t = jnp.transpose(jnp.broadcast_to(packed, (128, PD))).astype(jnp.int32)
    col_t = packed_t & 1023
    row_t = (packed_t >> 10) & 63
    lane_t = packed_t >> 16
    lanes = lax.broadcasted_iota(jnp.int32, (PD, 128), 1)
    lm[...] = jnp.where(lane_t == lanes, 1.0, 0.0)
    r[...] = jnp.where(row_t == lanes, 1.0, 0.0).astype(BF16)
    for j in range(CX):
        g[:, j * 128 : (j + 1) * 128] = jnp.where(col_t == lanes + 128 * j, 1.0, 0.0).astype(BF16)
    rows64 = lax.broadcasted_iota(jnp.int32, (64, PD), 0)
    a_t[...] = jnp.where(row == rows64, 1.0, 0.0).astype(BF16)

    def prep(x, state):
        p, sw, sg = state[0, x], state[1, x], state[2, x]
        m1, m2, m3, m4 = mobilities(p, sw, sg)
        q[0, x, 0:CY] = p
        q[1, x, 0:CY] = m1
        q[2, x, 0:CY] = m2
        q[3, x, 0:CY] = m3 + m4
        here = pl.ds(pl.multiple_of(x * CY, CY), CY)
        mixed = 0.8 * m1 + m2 + 0.15 * m3
        hi, lo = split(mixed)
        mlh[here, 0:128] = hi
        mll[here, 0:128] = lo
        hi, lo = split(total_mobility(sw, sg))
        mlh[here, 128:256] = hi
        mll[here, 128:256] = lo

    def well_sums(n):
        seen = jnp.dot(g[...], mlh[...], preferred_element_type=F32) + jnp.dot(
            g[...], mll[...], preferred_element_type=F32
        )
        num = jnp.sum(cf[...] * seen[:, 0:128], axis=1, keepdims=True)
        den = jnp.sum(cf[...] * seen[:, 128:256], axis=1, keepdims=True)
        spread = jnp.concatenate([lm[...] * num, lm[...] * den], axis=1)
        tb[n] = dot2(a_t[...], spread)

    def wait_bytes(ref, sem):
        pltpu.make_async_copy(ref, ref, sem).wait()

    def send_one(n):
        for k in (4, 3, 5, 2, 6, 1, 7):
            to = lax.rem(gy + k, NGY)
            pltpu.make_async_remote_copy(
                tb.at[n, pl.ds(pl.multiple_of(to * 8, 8), 8)], r1.at[n, k - 1],
                ph_send.at[n, 0], ph_recv.at[n, 0], device_id=(gx, to), device_id_type=MESH,
            ).start()

    def send_two(n):
        wait_bytes(r1.at[n], ph_recv.at[n, 0])
        x1[n] = tb[n, pl.ds(pl.multiple_of(gy * 8, 8), 8)] + jnp.sum(r1[n], axis=0)
        for k in (10, 9, 11, 6, 14, 2, 8, 5, 7, 13, 15, 1, 3, 4, 12):
            to = lax.rem(gx + k, NGX)
            pltpu.make_async_remote_copy(
                x1.at[n], r2.at[n, k - 1],
                ph_send.at[n, 1], ph_recv.at[n, 1], device_id=(to, gy), device_id_type=MESH,
            ).start()

    def send_three(n):
        wait_bytes(r2.at[n], ph_recv.at[n, 1])
        sums = x1[n] + jnp.sum(r2[n], axis=0)
        if n == 0:
            wait_bytes(wr, w_recv)
            w0[...] = w0[...] + jnp.sum(wr[...], axis=0)
        drop = w0[0:8]
        parent = w0[8:16]
        dens = (sums[:, 0:128] + 0.5) / (sums[:, 128:256] + 1.0)
        rise = dens * drop
        seg = lax.broadcasted_iota(jnp.int32, (8, 128), 0)
        press = jnp.where(seg == 0, parent + rise, rise)
        for above in range(7):
            hit = (seg > above) & (parent == float(above))
            press = press + jnp.where(hit, press[above : above + 1], 0.0)
        answer = jnp.concatenate([press, dens], axis=1)
        x3[n] = answer
        mine = pl.ds(pl.multiple_of(gy * 8, 8), 8)
        r3[n, mine] = answer
        for k in (4, 3, 5, 2, 6, 1, 7):
            to = lax.rem(gy + k, NGY)
            pltpu.make_async_remote_copy(
                x3.at[n], r3.at[n, mine],
                ph_send.at[n, 2], ph_recv.at[n, 2], device_id=(gx, to), device_id_type=MESH,
            ).start()
        return press

    def answers(n):
        wait_bytes(r3.at[n, pl.ds(0, 56)], ph_recv.at[n, 2])
        seen = dot2(r[:, 0:64], r3[n])
        press = jnp.sum(lm[...] * seen[:, 0:128], axis=1, keepdims=True)
        dens = jnp.sum(lm[...] * seen[:, 128:256], axis=1, keepdims=True)
        depth = (lax.broadcasted_iota(jnp.int32, (1, NZ), 1).astype(F32) + 0.5) / NZ - 0.5
        wl[...] = dot2(s[...], cf[...] * (press + (0.5 * dens) * depth))

    def pack_rows(state, rows, fields):
        for f in range(fields):
            for x in range(CX):
                rows[0, f, x : x + 1] = state[f, x, CY - 1 : CY]
                rows[1, f, x : x + 1] = state[f, x, 0:1]

    def halo_copies(n, state, planes, rows_out, rows_in, fields):
        up, down = lax.rem(gx + 1, NGX), lax.rem(gx + NGX - 1, NGX)
        right, left = lax.rem(gy + 1, NGY), lax.rem(gy + NGY - 1, NGY)
        four = (
            (state.at[pl.ds(0, fields), CX - 1], planes.at[0], (up, gy)),
            (state.at[pl.ds(0, fields), 0], planes.at[1], (down, gy)),
            (rows_out.at[0], rows_in.at[0], (gx, right)),
            (rows_out.at[1], rows_in.at[1], (gx, left)),
        )
        return [
            pltpu.make_async_remote_copy(
                src, dst, halo_send.at[n, i], halo_recv.at[n, i], device_id=to, device_id_type=MESH
            )
            for i, (src, dst, to) in enumerate(four)
        ]

    def inner_faces(x, c):
        for y0 in range(0, CY, YB):
            ys = slice(y0, y0 + YB)
            p, m1, m2, m34 = (q[f, x, ys] for f in range(4))
            n = [q[f, x + 1, ys] for f in range(4)]
            flow = side_flux(p, (m1, m2, m34), n[0], n[1:], tx[x, ys])
            acc = []
            for f in range(3):
                acc.append(flow[f] - fx[f, ys])
                fx[f, ys] = flow[f]
            n = [q[f, x, y0 + 1 : y0 + 1 + YB] for f in range(4)]
            flow = side_flux(p, (m1, m2, m34), n[0], n[1:], ty[x, ys])
            for f in range(3):
                fy[f, 8 + y0 : 8 + y0 + YB] = flow[f]
                acc[f] = acc[f] + (flow[f] - fy[f, 7 + y0 : 7 + y0 + YB])
            m4 = m1 * (0.2 * p)
            m3 = m34 - m4
            pn, n1, n2, n3, n4 = (pltpu.roll(v, NZ - 1, 1) for v in (p, m1, m2, m3, m4))
            d, total = p - pn, p + pn
            phi1 = d + (0.001 * total + 0.038)
            phi2 = d + (0.0005 * total + 0.049)
            phi3 = d + (0.003 * total + 0.0015)
            t = tz[x, ys]
            up1 = phi1 > 0.0
            t1 = t * phi1
            flow = (
                t1 * jnp.where(up1, m1, n1),
                (t * phi2) * jnp.where(phi2 > 0.0, m2, n2),
                (t * phi3) * jnp.where(phi3 > 0.0, m3, n3) + t1 * jnp.where(up1, m4, n4),
            )
            for f in range(3):
                acc[f] = acc[f] + (flow[f] - pltpu.roll(flow[f], 1, 1))
            sw, sg = c[1, x, ys], c[2, x, ys]
            stored1 = (0.95 + 0.05 * p) * (1.0 - sw - sg)
            stored2 = (0.98 + 0.02 * p) * sw
            stored3 = (0.2 + 0.8 * p) * sg + (0.2 * p) * stored1
            vol = pv[x, ys]
            for f, held in enumerate((stored1, stored2, stored3)):
                base[f, x, ys] = vol * held - mo[f, x, ys] + acc[f]

    def plane_faces(planes):
        for side, x in ((0, 0), (1, CX - 1)):
            ph = planes[side, 0]
            h1, h2, h3, h4 = mobilities(ph, planes[side, 1], planes[side, 2])
            there, here = (h1, h2, h3 + h4), [q[f, x, 0:CY] for f in (1, 2, 3)]
            p = q[0, x, 0:CY]
            if side == 0:
                flow = side_flux(ph, there, p, here, txb[0])
            else:
                flow = side_flux(p, here, ph, there, txb[1])
            for f in range(3):
                base[f, x] = base[f, x] - flow[f] if side == 0 else base[f, x] + flow[f]

    def row_faces(rows, rows_out):
        for side, y in ((0, 0), (1, CY - 1)):
            ph = rows[side, 0]
            h1, h2, h3, h4 = mobilities(ph, rows[side, 1], rows[side, 2])
            own_side = 1 - side
            p = rows_out[own_side, 0]
            m1, m2, m3, m4 = mobilities(p, rows_out[own_side, 1], rows_out[own_side, 2])
            there, here = (h1, h2, h3 + h4), (m1, m2, m3 + m4)
            if side == 0:
                flow = side_flux(ph, there, p, here, tyb[0])
            else:
                flow = side_flux(p, here, ph, there, tyb[1])
            for f in range(3):
                change = -flow[f] if side == 0 else flow[f]
                for x in range(CX):
                    base[f, x, y : y + 1] = base[f, x, y : y + 1] + change[x : x + 1]

    def transmissibility(x, c):
        k = st1[3, x]
        nxt = st1[3, jnp.minimum(x + 1, CX - 1)]
        tx[x] = harmonic(k, nxt) * jnp.where(x < CX - 1, 1.0, 0.0)
        ys = lax.broadcasted_iota(jnp.int32, (CY, NZ), 0)
        zs = lax.broadcasted_iota(jnp.int32, (CY, NZ), 1)
        ty[x] = jnp.where(ys == CY - 1, 0.0, harmonic(k, pltpu.roll(k, CY - 1, 0)))
        tz[x] = jnp.where(zs == NZ - 1, 0.0, 0.1 * harmonic(k, pltpu.roll(k, NZ - 1, 1)))
        return c

    def each_plane(body):
        def step(x, c):
            body(x)
            return c
        lax.fori_loop(0, CX, step, 0)

    for i in range(3):
        loads[i].wait()
    each_plane(lambda x: prep(x, st1))
    loads[3].wait()
    well_sums(0)
    pl.semaphore_wait(barrier, NGX - 1 + NGY - 1)
    send_one(0)

    eye = jnp.where(
        lax.broadcasted_iota(jnp.int32, (8, 8), 0) == lax.broadcasted_iota(jnp.int32, (8, 8), 1), 1.0, 0.0
    )
    place = jnp.where(
        lax.broadcasted_iota(jnp.int32, (8, 128), 0) + gx * 8 == lax.broadcasted_iota(jnp.int32, (8, 128), 1),
        1.0, 0.0,
    )
    flip = (((1,), (1,)), ((), ()))
    w0[0:8] = exact_dot(exact_dot(eye, drop_ref[...], flip), place)
    w0[8:16] = exact_dot(exact_dot(eye, par_ref[...].astype(F32), flip), place)
    w0[8:9] = exact_dot(bot_ref[...], place)
    w_copies = []
    for k in range(1, NGX):
        w_copies.append(pltpu.make_async_remote_copy(
            w0, wr.at[k - 1], w_send, w_recv,
            device_id=(lax.rem(gx + k, NGX), gy), device_id_type=MESH,
        ))
    for copy in w_copies:
        copy.start()

    loads[4].wait()
    pack_rows(st1, hys1, 4)
    halo_one = halo_copies(0, st1, hx1, hys1, hy1, 4)
    for copy in halo_one:
        copy.start()

    for f in range(4):
        q[f, CX] = jnp.zeros((CY + 8, NZ), F32)
        for x in range(CX):
            q[f, x, CY : CY + 8] = jnp.zeros((8, NZ), F32)
    for f in range(3):
        fx[f] = jnp.zeros((CY, NZ), F32)
        fy[f, 0:8] = jnp.zeros((8, NZ), F32)
    each_row = lax.broadcasted_iota(jnp.int32, (128, PD), 0)
    for j in range(CX):
        s[j * 128 : (j + 1) * 128] = jnp.where(col == each_row + 128 * j, 1.0, 0.0).astype(BF16)
    c0[...] = dot2(s[...], cf[...])
    for i in range(5, 8):
        loads[i].wait()
    wait_bytes(wr, w_send)
    send_two(0)
    lax.fori_loop(0, CX, transmissibility, 0)
    each_plane(lambda x: inner_faces(x, st1))
    send_three(0)
    for copy in halo_one:
        copy.wait()
    for side, x, there in ((0, 0, gx > 0), (1, CX - 1, gx < NGX - 1)):
        txb[side] = harmonic(hx1[side, 3], st1[3, x]) * jnp.where(there, 1.0, 0.0)
    for side, there in ((0, gy > 0), (1, gy < NGY - 1)):
        tyb[side] = harmonic(hy1[side, 3], hys1[1 - side, 3]) * jnp.where(there, 1.0, 0.0)
    plane_faces(hx1)
    row_faces(hy1, hys1)
    answers(0)

    def update(x):
        here = pl.ds(pl.multiple_of(x * CY, CY), CY)
        drive = q[0, x, 0:CY] * c0[here] - wl[here]
        for f in range(3):
            first = base[f, x] + q[f + 1, x, 0:CY] * drive
            st2[f, x] = st1[f, x] - ns[f, x] * first
        prep(x, st2)

    each_plane(update)
    well_sums(1)
    send_one(1)
    pack_rows(st2, hys2, 3)
    halo_two = halo_copies(1, st2, hx2, hys2, hy2, 3)
    for copy in halo_two:
        copy.start()
    for f in range(3):
        fx[f] = jnp.zeros((CY, NZ), F32)
    send_two(1)
    each_plane(lambda x: inner_faces(x, st2))
    press = send_three(1)
    press_ref[...] = exact_dot(place, press, flip)
    for copy in halo_two:
        copy.wait()
    plane_faces(hx2)
    row_faces(hy2, hys2)
    answers(1)

    def finish(x):
        here = pl.ds(pl.multiple_of(x * CY, CY), CY)
        drive = q[0, x, 0:CY] * c0[here] - wl[here]
        for f in range(3):
            out_ref[f, x] = base[f, x] + q[f + 1, x, 0:CY] * drive

    each_plane(finish)
    for n in range(2):
        wait_bytes(r1.at[n], ph_send.at[n, 0])
        wait_bytes(r2.at[n], ph_send.at[n, 1])
        wait_bytes(r3.at[n, pl.ds(0, 56)], ph_send.at[n, 2])


def shards(
    pressure, water_sat, gas_sat, mass_old, pore_volume, permeability, newton_scale, conn_factor,
    perf_column, perf_owner, perf_well, perf_segment, seg_parent, seg_drop, bottom_press,
):
    vmem = pl.BlockSpec(memory_space=pltpu.VMEM)
    hbm = pl.BlockSpec(memory_space=pl.ANY)
    cells = (CX, CY, NZ)
    dma = pltpu.SemaphoreType.DMA
    scratch = [
        pltpu.VMEM((4,) + cells, F32),
        pltpu.VMEM((3,) + cells, F32),
        pltpu.VMEM((PD, NZ), F32),
        pltpu.VMEM(cells, F32),
        pltpu.VMEM((3,) + cells, F32),
        pltpu.VMEM((3,) + cells, F32),
        pltpu.VMEM((2, 4, CY, NZ), F32),
        pltpu.VMEM((2, 3, CY, NZ), F32),
        pltpu.VMEM((2, 4, CX, NZ), F32),
        pltpu.VMEM((2, 3, CX, NZ), F32),
        pltpu.VMEM((2, 4, CX, NZ), F32),
        pltpu.VMEM((2, 3, CX, NZ), F32),
        pltpu.VMEM((4, CX + 1, CY + 8, NZ), F32),
        pltpu.VMEM(cells, F32),
        pltpu.VMEM(cells, F32),
        pltpu.VMEM(cells, F32),
        pltpu.VMEM((2, CY, NZ), F32),
        pltpu.VMEM((2, CX, NZ), F32),
        pltpu.VMEM((3, CY, NZ), F32),
        pltpu.VMEM((3, CY + 8, NZ), F32),
        pltpu.VMEM((3,) + cells, F32),
        pltpu.VMEM((COLS, NZ), F32),
        pltpu.VMEM((COLS, NZ), F32),
        pltpu.VMEM((PD, COLS), BF16),
        pltpu.VMEM((COLS, PD), BF16),
        pltpu.VMEM((64, PD), BF16),
        pltpu.VMEM((PD, 128), BF16),
        pltpu.VMEM((PD, 128), F32),
        pltpu.VMEM((COLS, 256), BF16),
        pltpu.VMEM((COLS, 256), BF16),
        pltpu.VMEM((2, 64, 256), F32),
        pltpu.VMEM((2, NGY - 1, 8, 256), F32),
        pltpu.VMEM((2, 8, 256), F32),
        pltpu.VMEM((2, NGX - 1, 8, 256), F32),
        pltpu.VMEM((2, 8, 256), F32),
        pltpu.VMEM((2, 64, 256), F32),
        pltpu.VMEM((16, 128), F32),
        pltpu.VMEM((NGX - 1, 16, 128), F32),
        dma((8,)), dma((2, 4)), dma((2, 4)), dma((2, 3)), dma((2, 3)), dma, dma,
    ]
    return pl.pallas_call(
        kernel,
        out_shape=(
            jax.ShapeDtypeStruct((3,) + cells, F32),
            jax.ShapeDtypeStruct((8, 8), F32),
        ),
        in_specs=[hbm] * 8 + [vmem] * 7,
        out_specs=(vmem, vmem),
        scratch_shapes=scratch,
        compiler_params=pltpu.CompilerParams(
            collective_id=0, has_side_effects=True, vmem_limit_bytes=48 << 20
        ),
    )(
        pressure, water_sat, gas_sat, mass_old, pore_volume, permeability, newton_scale, conn_factor,
        perf_column.reshape(1, PD), perf_owner.reshape(1, PD), perf_well.reshape(1, PD),
        perf_segment.reshape(1, PD), seg_parent, seg_drop, bottom_press.reshape(1, 8),
    )


def solution(mesh):
    cell = P("gx", "gy", None)
    triple = P(None, "gx", "gy", None)
    flat = P(("gx", "gy"))
    rows = P(("gx", "gy"), None)
    return jax.shard_map(
        shards,
        mesh=mesh,
        in_specs=(
            cell, cell, cell, triple, cell, cell, triple,
            rows, flat, rows, flat, flat, rows, rows, flat,
        ),
        out_specs=(triple, rows),
        check_vma=False,
    )
```

```python
import functools

import jax
import jax.numpy as jnp
from jax import lax
from jax.experimental import pallas as pl
from jax.experimental.pallas import tpu as pltpu
from jax.sharding import PartitionSpec as P

MESH = pl.DeviceIdType.MESH
F32 = jnp.float32
BF16 = jnp.bfloat16
NGX, NGY = 16, 8
CX, CY, NZ = 8, 128, 128
PD = 384
COLS = CX * CY
YB = 32
GX_ORDER = (10, 9, 11, 6, 14, 2, 8, 5, 7, 13, 15, 1, 3, 4, 12)
GY_ORDER = (4, 3, 5, 2, 6, 1, 7)


def split(v):
    hi = v.astype(BF16)
    return hi, (v - hi.astype(F32)).astype(BF16)


def dot2(one_hot, v):
    hi, lo = split(v)
    return jnp.dot(one_hot, hi, preferred_element_type=F32) + jnp.dot(
        one_hot, lo, preferred_element_type=F32
    )


def exact_dot(a, b, dims=(((1,), (0,)), ((), ()))):
    return lax.dot_general(a, b, dims, precision=lax.Precision.HIGHEST, preferred_element_type=F32)


def mobilities(p, sw, sg):
    so = 1.0 - sw - sg
    m1 = (0.5 * so * so) * (0.95 + 0.05 * p)
    m2 = (2.0 * sw * sw) * (0.98 + 0.02 * p)
    m3 = (5.0 * sg * sg) * (0.2 + 0.8 * p)
    m4 = m1 * (0.2 * p)
    return m1, m2, m3, m4


def total_mobility(sw, sg):
    so = 1.0 - sw - sg
    return 0.5 * so * so + 2.0 * sw * sw + 5.0 * sg * sg


def side_flux(p_i, m_i, p_j, m_j, trans):
    d = p_i - p_j
    up = d > 0.0
    t = trans * d
    return [t * jnp.where(up, a, b) for a, b in zip(m_i, m_j)]


def harmonic(a, b):
    return 2.0 * a * b / (a + b)


def kernel(
    p_h, sw_h, sg_h, mo_h, pv_h, k_h, ns_h, cf_h,
    col_h, own_h, well_h, seg_h, par_h, drop_h, bot_h,
    out_ref, press_ref,
    st1, st2, cf, pv, mo, ns, hx1, hx2, hy1, hy2, hys1, hys2,
    hk, q, tx, ty, tz, txb, tyb, fx, fy, base, c0, wl,
    g, s, a_t, r, lm, mlh, mll, same, ct, edge, dh, dl, gq, eh, el, vhl,
    tb, r1, x1, r2, y1, r4, x3, r3, wd,
    col_ref, own_ref, well_ref, seg_ref, par_ref, drop_ref, bot_ref,
    small_sem, load_sem, halo_send, halo_recv, k_send, k_recv, ph_send, ph_recv,
):
    gx = lax.axis_index("gx")
    gy = lax.axis_index("gy")

    small = [
        pltpu.make_async_copy(src, dst, small_sem.at[i])
        for i, (src, dst) in enumerate((
            (col_h, col_ref), (own_h, own_ref), (well_h, well_ref), (seg_h, seg_ref),
            (par_h, par_ref), (drop_h, drop_ref), (bot_h, bot_ref),
        ))
    ]
    for load in small:
        load.start()
    loads = [
        pltpu.make_async_copy(p_h, st1.at[0], load_sem.at[0]),
        pltpu.make_async_copy(sw_h, st1.at[1], load_sem.at[1]),
        pltpu.make_async_copy(sg_h, st1.at[2], load_sem.at[2]),
        pltpu.make_async_copy(cf_h, cf, load_sem.at[3]),
        pltpu.make_async_copy(k_h, st1.at[3], load_sem.at[4]),
        pltpu.make_async_copy(pv_h, pv, load_sem.at[5]),
        pltpu.make_async_copy(mo_h, mo, load_sem.at[6]),
        pltpu.make_async_copy(ns_h, ns, load_sem.at[7]),
    ]
    for load in loads[:4]:
        load.start()

    barrier = pltpu.get_barrier_semaphore()
    for k in GX_ORDER:
        pl.semaphore_signal(barrier, 1, device_id=(lax.rem(gx + k, NGX), gy), device_id_type=MESH)
    for k in GY_ORDER:
        pl.semaphore_signal(barrier, 1, device_id=(gx, lax.rem(gy + k, NGY)), device_id_type=MESH)

    for load in small:
        load.wait()
    col = col_ref[...].reshape(1, PD)
    own = own_ref[...]
    row = lax.rem(own, NGY) * 8 + seg_ref[...].reshape(1, PD)
    lane = (own // NGY) * 8 + well_ref[...].reshape(1, PD)
    packed = (col + 1024 * row + 65536 * lane).astype(F32)
    packed_t = jnp.transpose(jnp.broadcast_to(packed, (128, PD))).astype(jnp.int32)
    col_t = packed_t & 1023
    row_t = (packed_t >> 10) & 63
    lane_t = packed_t >> 16
    lanes = lax.broadcasted_iota(jnp.int32, (PD, 128), 1)
    ct[...] = col_t
    lm[...] = jnp.where(lane_t == lanes, 1.0, 0.0)
    r[...] = jnp.where(row_t == lanes, 1.0, 0.0).astype(BF16)
    for j in range(CX):
        g[:, j * 128 : (j + 1) * 128] = jnp.where(col_t == lanes + 128 * j, 1.0, 0.0).astype(BF16)
    rows64 = lax.broadcasted_iota(jnp.int32, (64, PD), 0)
    a_t[...] = jnp.where(row == rows64, 1.0, 0.0).astype(BF16)

    def prep(x, state, sums):
        p, sw, sg = state[0, x], state[1, x], state[2, x]
        m1, m2, m3, m4 = mobilities(p, sw, sg)
        q[0, x, 0:CY] = p
        q[1, x, 0:CY] = m1
        q[2, x, 0:CY] = m2
        q[3, x, 0:CY] = m3 + m4
        if not sums:
            return
        here = pl.ds(pl.multiple_of(x * CY, CY), CY)
        mixed = 0.8 * m1 + m2 + 0.15 * m3
        hi, lo = split(mixed)
        mlh[here, 0:128] = hi
        mll[here, 0:128] = lo
        hi, lo = split(total_mobility(sw, sg))
        mlh[here, 128:256] = hi
        mll[here, 128:256] = lo

    def well_sums(n, mixed, total):
        num = jnp.sum(cf[...] * mixed, axis=1, keepdims=True)
        den = jnp.sum(cf[...] * total, axis=1, keepdims=True)
        spread = jnp.concatenate([lm[...] * num, lm[...] * den], axis=1)
        tb[n] = dot2(a_t[...], spread)

    def wait_bytes(ref, sem):
        pltpu.make_async_copy(ref, ref, sem).wait()

    out_parts = (x1, y1)
    in_parts = (r2, r4)

    def send_one(n):
        for k in GY_ORDER:
            to = lax.rem(gy + k, NGY)
            pltpu.make_async_remote_copy(
                tb.at[n, pl.ds(pl.multiple_of(to * 8, 8), 8)], r1.at[n, k - 1],
                ph_send.at[n, 0], ph_recv.at[n, 0], device_id=(gx, to), device_id_type=MESH,
            ).start()

    def send_two(n):
        wait_bytes(r1.at[n], ph_recv.at[n, 0])
        part = tb[n, pl.ds(pl.multiple_of(gy * 8, 8), 8)] + jnp.sum(r1[n], axis=0)
        if n == 0:
            x1[:, 0:256] = part
        else:
            y1[...] = part
        for k in GX_ORDER:
            to = lax.rem(gx + k, NGX)
            pltpu.make_async_remote_copy(
                out_parts[n], in_parts[n].at[k - 1],
                ph_send.at[n, 1], ph_recv.at[n, 1], device_id=(to, gy), device_id_type=MESH,
            ).start()

    def send_three(n):
        wait_bytes(in_parts[n], ph_recv.at[n, 1])
        sums = out_parts[n][...] + jnp.sum(in_parts[n][...], axis=0)
        if n == 0:
            wd[...] = sums[:, 256:512]
        drop = wd[:, 0:128]
        parent = wd[:, 128:256]
        dens = (sums[:, 0:128] + 0.5) / (sums[:, 128:256] + 1.0)
        rise = dens * drop
        seg = lax.broadcasted_iota(jnp.int32, (8, 128), 0)
        press = jnp.where(seg == 0, parent + rise, rise)
        for above in range(7):
            hit = (seg > above) & (parent == float(above))
            press = press + jnp.where(hit, press[above : above + 1], 0.0)
        answer = jnp.concatenate([press, dens], axis=1)
        x3[n] = answer
        mine = pl.ds(pl.multiple_of(gy * 8, 8), 8)
        r3[n, mine] = answer
        for k in GY_ORDER:
            to = lax.rem(gy + k, NGY)
            pltpu.make_async_remote_copy(
                x3.at[n], r3.at[n, mine],
                ph_send.at[n, 2], ph_recv.at[n, 2], device_id=(gx, to), device_id_type=MESH,
            ).start()
        return press

    def answers(n):
        wait_bytes(r3.at[n, pl.ds(0, 56)], ph_recv.at[n, 2])
        seen = dot2(r[:, 0:64], r3[n])
        press = jnp.sum(lm[...] * seen[:, 0:128], axis=1, keepdims=True)
        dens = jnp.sum(lm[...] * seen[:, 128:256], axis=1, keepdims=True)
        depth = (lax.broadcasted_iota(jnp.int32, (1, NZ), 1).astype(F32) + 0.5) / NZ - 0.5
        hi, lo = split(cf[...] * (press + (0.5 * dens) * depth))
        vhl[:, 0:128] = hi
        vhl[:, 128:256] = lo

    def spread_answers():
        both = jnp.dot(s[...], vhl[...], preferred_element_type=F32)
        wl[...] = both[:, 0:128] + both[:, 128:256]

    def pack_rows(state, rows, fields):
        for f in range(fields):
            for x in range(CX):
                rows[0, f, x : x + 1] = state[f, x, CY - 1 : CY]
                rows[1, f, x : x + 1] = state[f, x, 0:1]

    def halo_copies(n, state, planes, rows_out, rows_in):
        up, down = lax.rem(gx + 1, NGX), lax.rem(gx + NGX - 1, NGX)
        right, left = lax.rem(gy + 1, NGY), lax.rem(gy + NGY - 1, NGY)
        four = (
            (state.at[pl.ds(0, 3), CX - 1], planes.at[0], (up, gy)),
            (state.at[pl.ds(0, 3), 0], planes.at[1], (down, gy)),
            (rows_out.at[0], rows_in.at[0], (gx, right)),
            (rows_out.at[1], rows_in.at[1], (gx, left)),
        )
        return [
            pltpu.make_async_remote_copy(
                src, dst, halo_send.at[n, i], halo_recv.at[n, i], device_id=to, device_id_type=MESH
            )
            for i, (src, dst, to) in enumerate(four)
        ]

    def inner_faces(x, c):
        for y0 in range(0, CY, YB):
            ys = slice(y0, y0 + YB)
            p, m1, m2, m34 = (q[f, x, ys] for f in range(4))
            n = [q[f, x + 1, ys] for f in range(4)]
            flow = side_flux(p, (m1, m2, m34), n[0], n[1:], tx[x, ys])
            acc = []
            for f in range(3):
                acc.append(flow[f] - fx[f, ys])
                fx[f, ys] = flow[f]
            n = [q[f, x, y0 + 1 : y0 + 1 + YB] for f in range(4)]
            flow = side_flux(p, (m1, m2, m34), n[0], n[1:], ty[x, ys])
            for f in range(3):
                fy[f, 8 + y0 : 8 + y0 + YB] = flow[f]
                acc[f] = acc[f] + (flow[f] - fy[f, 7 + y0 : 7 + y0 + YB])
            m4 = m1 * (0.2 * p)
            m3 = m34 - m4
            pn, n1, n2, n3, n4 = (pltpu.roll(v, NZ - 1, 1) for v in (p, m1, m2, m3, m4))
            d, total = p - pn, p + pn
            phi1 = d + (0.001 * total + 0.038)
            phi2 = d + (0.0005 * total + 0.049)
            phi3 = d + (0.003 * total + 0.0015)
            t = tz[x, ys]
            up1 = phi1 > 0.0
            t1 = t * phi1
            flow = (
                t1 * jnp.where(up1, m1, n1),
                (t * phi2) * jnp.where(phi2 > 0.0, m2, n2),
                (t * phi3) * jnp.where(phi3 > 0.0, m3, n3) + t1 * jnp.where(up1, m4, n4),
            )
            for f in range(3):
                acc[f] = acc[f] + (flow[f] - pltpu.roll(flow[f], 1, 1))
            sw, sg = c[1, x, ys], c[2, x, ys]
            stored1 = (0.95 + 0.05 * p) * (1.0 - sw - sg)
            stored2 = (0.98 + 0.02 * p) * sw
            stored3 = (0.2 + 0.8 * p) * sg + (0.2 * p) * stored1
            vol = pv[x, ys]
            for f, held in enumerate((stored1, stored2, stored3)):
                base[f, x, ys] = vol * held - mo[f, x, ys] + acc[f]

    def put_edge(start, size, f, change):
        hi, lo = split(change)
        eh[start : start + size, f * 128 : (f + 1) * 128] = hi
        el[start : start + size, f * 128 : (f + 1) * 128] = lo

    def plane_faces(planes, edges):
        for side, x in ((0, 0), (1, CX - 1)):
            ph = planes[side, 0]
            h1, h2, h3, h4 = mobilities(ph, planes[side, 1], planes[side, 2])
            there, here = (h1, h2, h3 + h4), [q[f, x, 0:CY] for f in (1, 2, 3)]
            p = q[0, x, 0:CY]
            if side == 0:
                flow = side_flux(ph, there, p, here, txb[0])
            else:
                flow = side_flux(p, here, ph, there, txb[1])
            for f in range(3):
                base[f, x] = base[f, x] - flow[f] if side == 0 else base[f, x] + flow[f]
                if edges:
                    change = ns[f, x] * flow[f] if side == 0 else -ns[f, x] * flow[f]
                    put_edge(side * CY, CY, f, change)

    def row_faces(rows, rows_out, edges):
        row_edges = []
        for side, y in ((0, 0), (1, CY - 1)):
            ph = rows[side, 0]
            h1, h2, h3, h4 = mobilities(ph, rows[side, 1], rows[side, 2])
            own_side = 1 - side
            p = rows_out[own_side, 0]
            m1, m2, m3, m4 = mobilities(p, rows_out[own_side, 1], rows_out[own_side, 2])
            there, here = (h1, h2, h3 + h4), (m1, m2, m3 + m4)
            if side == 0:
                flow = side_flux(ph, there, p, here, tyb[0])
            else:
                flow = side_flux(p, here, ph, there, tyb[1])
            for f in range(3):
                change = -flow[f] if side == 0 else flow[f]
                for x in range(CX):
                    base[f, x, y : y + 1] = base[f, x, y : y + 1] + change[x : x + 1]
                if edges:
                    scale = jnp.concatenate([ns[f, x, y : y + 1] for x in range(CX)], axis=0)
                    row_edges.append((f, -scale * change))
        if edges:
            for f in range(3):
                put_edge(2 * CY, 16, f, jnp.concatenate([v for i, v in row_edges if i == f], axis=0))

    def transmissibility(x, c):
        k = st1[3, x]
        nxt = st1[3, jnp.minimum(x + 1, CX - 1)]
        tx[x] = harmonic(k, nxt) * jnp.where(x < CX - 1, 1.0, 0.0)
        ys = lax.broadcasted_iota(jnp.int32, (CY, NZ), 0)
        zs = lax.broadcasted_iota(jnp.int32, (CY, NZ), 1)
        ty[x] = jnp.where(ys == CY - 1, 0.0, harmonic(k, pltpu.roll(k, CY - 1, 0)))
        tz[x] = jnp.where(zs == NZ - 1, 0.0, 0.1 * harmonic(k, pltpu.roll(k, NZ - 1, 1)))
        return c

    def each_plane(body):
        def step(x, c):
            body(x)
            return c
        lax.fori_loop(0, CX, step, 0)

    def wells_data():
        eye = jnp.where(
            lax.broadcasted_iota(jnp.int32, (8, 8), 0) == lax.broadcasted_iota(jnp.int32, (8, 8), 1), 1.0, 0.0
        )
        x1[:, 256:384] = exact_dot(exact_dot(eye, drop_ref[...], flip), place)
        parent = exact_dot(exact_dot(eye, par_ref[...].astype(F32), flip), place)
        bottom = exact_dot(bot_ref[...].reshape(1, 8), place)
        x1[:, 384:512] = jnp.where(lax.broadcasted_iota(jnp.int32, (8, 128), 0) == 0, bottom, parent)

    def column_fields(x):
        here = pl.ds(pl.multiple_of(x * CY, CY), CY)
        fields = [st1[f, x] - ns[f, x] * base[f, x] for f in range(3)]
        fields += [ns[f, x] * q[f + 1, x, 0:CY] for f in range(3)]
        fields.append(q[0, x, 0:CY] * c0[here])
        for f, field in enumerate(fields):
            hi, lo = split(field)
            dh[here, f * 128 : (f + 1) * 128] = hi
            dl[here, f * 128 : (f + 1) * 128] = lo

    place = jnp.where(
        lax.broadcasted_iota(jnp.int32, (8, 128), 0) + gx * 8 == lax.broadcasted_iota(jnp.int32, (8, 128), 1),
        1.0, 0.0,
    )
    flip = (((1,), (1,)), ((), ()))

    for i in range(3):
        loads[i].wait()
    for load in loads[4:]:
        load.start()
    each_plane(lambda x: prep(x, st1, True))
    loads[4].wait()
    pl.semaphore_wait(barrier, NGX - 1 + NGY - 1)
    k_copies = [
        pltpu.make_async_remote_copy(
            st1.at[3, x], hk.at[i], k_send.at[i], k_recv.at[i],
            device_id=(lax.rem(gx + step, NGX), gy), device_id_type=MESH,
        )
        for i, (x, step) in enumerate(((CX - 1, 1), (0, NGX - 1)))
    ]
    halo_one = halo_copies(0, st1, hx1, hys1, hy1)
    for copy in halo_one[:2] + k_copies:
        copy.start()
    loads[3].wait()
    seen = jnp.dot(g[...], mlh[...], preferred_element_type=F32) + jnp.dot(
        g[...], mll[...], preferred_element_type=F32
    )
    well_sums(0, seen[:, 0:128], seen[:, 128:256])
    send_one(0)

    wells_data()
    pack_rows(st1, hys1, 4)
    for f in range(4):
        q[f, CX] = jnp.zeros((CY + 8, NZ), F32)
        for x in range(CX):
            q[f, x, CY : CY + 8] = jnp.zeros((8, NZ), F32)
    for f in range(3):
        fx[f] = jnp.zeros((CY, NZ), F32)
        fy[f, 0:8] = jnp.zeros((8, NZ), F32)
    each_row = lax.broadcasted_iota(jnp.int32, (128, PD), 0)
    for j in range(CX):
        s[j * 128 : (j + 1) * 128] = jnp.where(col == each_row + 128 * j, 1.0, 0.0).astype(BF16)
    here_t = ct[...]
    for j in range(3):
        same[:, j * 128 : (j + 1) * 128] = jnp.where(
            here_t == col[:, j * 128 : (j + 1) * 128], 1.0, 0.0
        ).astype(BF16)
    edge[:, 0:128] = g[:, 0:128]
    edge[:, 128:256] = g[:, COLS - 128 : COLS]
    spot = jnp.where(lanes < 8, lanes * 128, (lanes - 8) * 128 + 127)
    edge[:, 256:384] = jnp.where((here_t == spot) & (lanes < 16), 1.0, 0.0).astype(BF16)
    eh[256:384] = jnp.zeros((128, 384), BF16)
    el[256:384] = jnp.zeros((128, 384), BF16)
    hi, lo = split(cf[...])
    both = jnp.dot(s[...], jnp.concatenate([hi, lo], axis=1), preferred_element_type=F32)
    c0[...] = both[:, 0:128] + both[:, 128:256]
    lax.fori_loop(0, CX, transmissibility, 0)
    send_two(0)
    for copy in halo_one[2:]:
        copy.start()

    for i in range(5, 8):
        loads[i].wait()
    each_plane(lambda x: inner_faces(x, st1))
    each_plane(column_fields)
    gq[...] = jnp.dot(g[...], dh[...], preferred_element_type=F32) + jnp.dot(
        g[...], dl[...], preferred_element_type=F32
    )
    send_three(0)

    for copy in k_copies + halo_one:
        copy.wait()
    for side, x, there in ((0, 0, gx > 0), (1, CX - 1, gx < NGX - 1)):
        txb[side] = harmonic(hk[side], st1[3, x]) * jnp.where(there, 1.0, 0.0)
    for side, there in ((0, gy > 0), (1, gy < NGY - 1)):
        tyb[side] = harmonic(hy1[side, 3], hys1[1 - side, 3]) * jnp.where(there, 1.0, 0.0)
    plane_faces(hx1, True)
    row_faces(hy1, hys1, True)
    gq[:, 0:384] = gq[:, 0:384] + (
        jnp.dot(edge[...], eh[...], preferred_element_type=F32)
        + jnp.dot(edge[...], el[...], preferred_element_type=F32)
    )
    answers(0)

    both = jnp.dot(same[...], vhl[...], preferred_element_type=F32)
    drive = gq[:, 768:896] - (both[:, 0:128] + both[:, 128:256])
    p, sw, sg = (gq[:, f * 128 : (f + 1) * 128] - gq[:, (f + 3) * 128 : (f + 4) * 128] * drive for f in range(3))
    m1, m2, m3, m4 = mobilities(p, sw, sg)
    well_sums(1, 0.8 * m1 + m2 + 0.15 * m3, total_mobility(sw, sg))
    send_one(1)
    spread_answers()

    def update(x):
        here = pl.ds(pl.multiple_of(x * CY, CY), CY)
        drive = q[0, x, 0:CY] * c0[here] - wl[here]
        for f in range(3):
            first = base[f, x] + q[f + 1, x, 0:CY] * drive
            st2[f, x] = st1[f, x] - ns[f, x] * first
        prep(x, st2, False)

    each_plane(update)
    pack_rows(st2, hys2, 3)
    halo_two = halo_copies(1, st2, hx2, hys2, hy2)
    for f in range(3):
        fx[f] = jnp.zeros((CY, NZ), F32)
    send_two(1)
    for copy in halo_two:
        copy.start()
    each_plane(lambda x: inner_faces(x, st2))
    press = send_three(1)
    press_ref[...] = exact_dot(place, press, flip)
    for copy in halo_two:
        copy.wait()
    plane_faces(hx2, False)
    row_faces(hy2, hys2, False)
    answers(1)
    spread_answers()

    def finish(x):
        here = pl.ds(pl.multiple_of(x * CY, CY), CY)
        drive = q[0, x, 0:CY] * c0[here] - wl[here]
        for f in range(3):
            out_ref[f, x] = base[f, x] + q[f + 1, x, 0:CY] * drive

    each_plane(finish)
    for n in range(2):
        wait_bytes(r1.at[n], ph_send.at[n, 0])
        wait_bytes(in_parts[n], ph_send.at[n, 1])
        wait_bytes(r3.at[n, pl.ds(0, 56)], ph_send.at[n, 2])


def write_out(held, press, out, press_out, sem):
    copies = [pltpu.make_async_copy(held.at[f], out.at[f], sem.at[f]) for f in range(3)]
    copies.append(pltpu.make_async_copy(press, press_out, sem.at[3]))
    for copy in copies:
        copy.start()
    for copy in copies:
        copy.wait()


def shards(
    pressure, water_sat, gas_sat, mass_old, pore_volume, permeability, newton_scale, conn_factor,
    perf_column, perf_owner, perf_well, perf_segment, seg_parent, seg_drop, bottom_press,
):
    vmem = pl.BlockSpec(memory_space=pltpu.VMEM)
    hbm = pl.BlockSpec(memory_space=pltpu.HBM)
    cells = (CX, CY, NZ)
    dma = pltpu.SemaphoreType.DMA
    scratch = [
        pltpu.VMEM((4,) + cells, F32),
        pltpu.VMEM((3,) + cells, F32),
        pltpu.VMEM((PD, NZ), F32),
        pltpu.VMEM(cells, F32),
        pltpu.VMEM((3,) + cells, F32),
        pltpu.VMEM((3,) + cells, F32),
        pltpu.VMEM((2, 3, CY, NZ), F32),
        pltpu.VMEM((2, 3, CY, NZ), F32),
        pltpu.VMEM((2, 4, CX, NZ), F32),
        pltpu.VMEM((2, 3, CX, NZ), F32),
        pltpu.VMEM((2, 4, CX, NZ), F32),
        pltpu.VMEM((2, 3, CX, NZ), F32),
        pltpu.VMEM((2, CY, NZ), F32),
        pltpu.VMEM((4, CX + 1, CY + 8, NZ), F32),
        pltpu.VMEM(cells, F32),
        pltpu.VMEM(cells, F32),
        pltpu.VMEM(cells, F32),
        pltpu.VMEM((2, CY, NZ), F32),
        pltpu.VMEM((2, CX, NZ), F32),
        pltpu.VMEM((3, CY, NZ), F32),
        pltpu.VMEM((3, CY + 8, NZ), F32),
        pltpu.VMEM((3,) + cells, F32),
        pltpu.VMEM((COLS, NZ), F32),
        pltpu.VMEM((COLS, NZ), F32),
        pltpu.VMEM((PD, COLS), BF16),
        pltpu.VMEM((COLS, PD), BF16),
        pltpu.VMEM((64, PD), BF16),
        pltpu.VMEM((PD, 128), BF16),
        pltpu.VMEM((PD, 128), F32),
        pltpu.VMEM((COLS, 256), BF16),
        pltpu.VMEM((COLS, 256), BF16),
        pltpu.VMEM((PD, PD), BF16),
        pltpu.VMEM((PD, 128), jnp.int32),
        pltpu.VMEM((PD, 384), BF16),
        pltpu.VMEM((COLS, 896), BF16),
        pltpu.VMEM((COLS, 896), BF16),
        pltpu.VMEM((PD, 896), F32),
        pltpu.VMEM((384, 384), BF16),
        pltpu.VMEM((384, 384), BF16),
        pltpu.VMEM((PD, 256), BF16),
        pltpu.VMEM((2, 64, 256), F32),
        pltpu.VMEM((2, NGY - 1, 8, 256), F32),
        pltpu.VMEM((8, 512), F32),
        pltpu.VMEM((NGX - 1, 8, 512), F32),
        pltpu.VMEM((8, 256), F32),
        pltpu.VMEM((NGX - 1, 8, 256), F32),
        pltpu.VMEM((2, 8, 256), F32),
        pltpu.VMEM((2, 64, 256), F32),
        pltpu.VMEM((8, 256), F32),
        pltpu.VMEM((PD,), jnp.int32),
        pltpu.VMEM((1, PD), jnp.int32),
        pltpu.VMEM((PD,), jnp.int32),
        pltpu.VMEM((PD,), jnp.int32),
        pltpu.VMEM((8, 8), jnp.int32),
        pltpu.VMEM((8, 8), F32),
        pltpu.VMEM((8,), F32),
        dma((7,)), dma((8,)), dma((2, 4)), dma((2, 4)), dma((2,)), dma((2,)), dma((2, 3)), dma((2, 3)),
    ]
    fields = (
        pressure, water_sat, gas_sat, mass_old, pore_volume, permeability, newton_scale, conn_factor,
        perf_column, perf_owner.reshape(1, PD), perf_well, perf_segment, seg_parent, seg_drop, bottom_press,
    )
    results = pl.pallas_call(
        kernel,
        out_shape=(pltpu.VMEM((3,) + cells, F32), pltpu.VMEM((8, 8), F32)),
        in_specs=[hbm] * 15,
        out_specs=(vmem, vmem),
        scratch_shapes=scratch,
        compiler_params=pltpu.CompilerParams(
            collective_id=0, has_side_effects=True, vmem_limit_bytes=40 << 20
        ),
    )(*[pltpu.with_memory_space_constraint(v, pltpu.HBM) for v in fields])
    return pl.pallas_call(
        write_out,
        out_shape=(jax.ShapeDtypeStruct((3,) + cells, F32), jax.ShapeDtypeStruct((8, 8), F32)),
        in_specs=[vmem, vmem],
        out_specs=(hbm, hbm),
        scratch_shapes=[dma((4,))],
        compiler_params=pltpu.CompilerParams(vmem_limit_bytes=1 << 20),
    )(*[pltpu.with_memory_space_constraint(v, pltpu.VMEM) for v in results])


def solution(mesh):
    cell = P("gx", "gy", None)
    triple = P(None, "gx", "gy", None)
    flat = P(("gx", "gy"))
    rows = P(("gx", "gy"), None)
    return jax.shard_map(
        shards,
        mesh=mesh,
        in_specs=(
            cell, cell, cell, triple, cell, cell, triple,
            rows, flat, rows, flat, flat, rows, rows, flat,
        ),
        out_specs=(triple, rows),
        check_vma=False,
    )
```

```python
import functools

import jax
import jax.numpy as jnp
from jax import lax
from jax.experimental import pallas as pl
from jax.experimental.pallas import tpu as pltpu
from jax.sharding import PartitionSpec as P

MESH = pl.DeviceIdType.MESH
F32 = jnp.float32
BF16 = jnp.bfloat16
NGX, NGY = 16, 8
CX, CY, NZ = 8, 128, 128
PD = 384
COLS = CX * CY
YB = 32
GX_ORDER = (10, 9, 11, 6, 14, 2, 8, 5, 7, 13, 15, 1, 3, 4, 12)
GY_ORDER = (4, 3, 5, 2, 6, 1, 7)


def split(v):
    hi = v.astype(BF16)
    return hi, (v - hi.astype(F32)).astype(BF16)


def dot2(one_hot, v):
    hi, lo = split(v)
    return jnp.dot(one_hot, hi, preferred_element_type=F32) + jnp.dot(
        one_hot, lo, preferred_element_type=F32
    )


def exact_dot(a, b, dims=(((1,), (0,)), ((), ()))):
    return lax.dot_general(a, b, dims, precision=lax.Precision.HIGHEST, preferred_element_type=F32)


def mobilities(p, sw, sg):
    so = 1.0 - sw - sg
    m1 = (0.5 * so * so) * (0.95 + 0.05 * p)
    m2 = (2.0 * sw * sw) * (0.98 + 0.02 * p)
    m3 = (5.0 * sg * sg) * (0.2 + 0.8 * p)
    m4 = m1 * (0.2 * p)
    return m1, m2, m3, m4


def total_mobility(sw, sg):
    so = 1.0 - sw - sg
    return 0.5 * so * so + 2.0 * sw * sw + 5.0 * sg * sg


def side_flux(p_i, m_i, p_j, m_j, trans):
    d = p_i - p_j
    up = d > 0.0
    t = trans * d
    return [t * jnp.where(up, a, b) for a, b in zip(m_i, m_j)]


def harmonic(a, b):
    return 2.0 * a * b / (a + b)


def kernel(
    p_h, sw_h, sg_h, mo_h, pv_h, k_h, ns_h, cf_h,
    col_h, own_h, well_h, seg_h, par_h, drop_h, bot_h,
    base, q, s, vhl, press_ref,
    st1, st2, cf, pv, mo, ns, hx1, hx2, hy1, hy2, hys1, hys2,
    hk, tx, ty, tz, txb, tyb, fx, fy, c0, wl,
    g, a_t, r, lm, mlh, mll, same, ct, edge, dh, dl, gq, eh, el,
    tb, r1, x1, r2, y1, r4, x3, r3, w0, wr, wd,
    col_ref, own_ref, well_ref, seg_ref, par_ref, drop_ref, bot_ref,
    small_sem, load_sem, halo_send, halo_recv, k_send, k_recv, w_send, w_recv, ph_send, ph_recv,
):
    gx = lax.axis_index("gx")
    gy = lax.axis_index("gy")

    small = [
        pltpu.make_async_copy(src, dst, small_sem.at[i])
        for i, (src, dst) in enumerate((
            (col_h, col_ref), (own_h, own_ref), (well_h, well_ref), (seg_h, seg_ref),
            (par_h, par_ref), (drop_h, drop_ref), (bot_h, bot_ref),
        ))
    ]
    for load in small:
        load.start()
    loads = [
        pltpu.make_async_copy(p_h, st1.at[0], load_sem.at[0]),
        pltpu.make_async_copy(sw_h, st1.at[1], load_sem.at[1]),
        pltpu.make_async_copy(sg_h, st1.at[2], load_sem.at[2]),
        pltpu.make_async_copy(cf_h, cf, load_sem.at[3]),
        pltpu.make_async_copy(k_h, st1.at[3], load_sem.at[4]),
        pltpu.make_async_copy(pv_h, pv, load_sem.at[5]),
        pltpu.make_async_copy(mo_h, mo, load_sem.at[6]),
        pltpu.make_async_copy(ns_h, ns, load_sem.at[7]),
    ]
    for load in loads[:4]:
        load.start()

    barrier = pltpu.get_barrier_semaphore()
    for k in GX_ORDER:
        pl.semaphore_signal(barrier, 1, device_id=(lax.rem(gx + k, NGX), gy), device_id_type=MESH)
    for k in GY_ORDER:
        pl.semaphore_signal(barrier, 1, device_id=(gx, lax.rem(gy + k, NGY)), device_id_type=MESH)

    for load in small:
        load.wait()
    col = col_ref[...].reshape(1, PD)
    own = own_ref[...]
    row = lax.rem(own, NGY) * 8 + seg_ref[...].reshape(1, PD)
    lane = (own // NGY) * 8 + well_ref[...].reshape(1, PD)
    packed = (col + 1024 * row + 65536 * lane).astype(F32)
    packed_t = jnp.transpose(jnp.broadcast_to(packed, (128, PD))).astype(jnp.int32)
    col_t = packed_t & 1023
    row_t = (packed_t >> 10) & 63
    lane_t = packed_t >> 16
    lanes = lax.broadcasted_iota(jnp.int32, (PD, 128), 1)
    ct[...] = col_t
    lm[...] = jnp.where(lane_t == lanes, 1.0, 0.0)
    r[...] = jnp.where(row_t == lanes, 1.0, 0.0).astype(BF16)
    for j in range(CX):
        g[:, j * 128 : (j + 1) * 128] = jnp.where(col_t == lanes + 128 * j, 1.0, 0.0).astype(BF16)
    rows64 = lax.broadcasted_iota(jnp.int32, (64, PD), 0)
    a_t[...] = jnp.where(row == rows64, 1.0, 0.0).astype(BF16)

    def prep(x, state, sums):
        p, sw, sg = state[0, x], state[1, x], state[2, x]
        m1, m2, m3, m4 = mobilities(p, sw, sg)
        q[0, x, 0:CY] = p
        q[1, x, 0:CY] = m1
        q[2, x, 0:CY] = m2
        q[3, x, 0:CY] = m3 + m4
        if not sums:
            return
        here = pl.ds(pl.multiple_of(x * CY, CY), CY)
        mixed = 0.8 * m1 + m2 + 0.15 * m3
        hi, lo = split(mixed)
        mlh[here, 0:128] = hi
        mll[here, 0:128] = lo
        hi, lo = split(total_mobility(sw, sg))
        mlh[here, 128:256] = hi
        mll[here, 128:256] = lo

    def well_sums(n, mixed, total):
        num = jnp.sum(cf[...] * mixed, axis=1, keepdims=True)
        den = jnp.sum(cf[...] * total, axis=1, keepdims=True)
        spread = jnp.concatenate([lm[...] * num, lm[...] * den], axis=1)
        tb[n] = dot2(a_t[...], spread)

    def wait_bytes(ref, sem):
        pltpu.make_async_copy(ref, ref, sem).wait()

    out_parts = (x1, y1)
    in_parts = (r2, r4)

    def send_one(n):
        for k in GY_ORDER:
            to = lax.rem(gy + k, NGY)
            pltpu.make_async_remote_copy(
                tb.at[n, pl.ds(pl.multiple_of(to * 8, 8), 8)], r1.at[n, k - 1],
                ph_send.at[n, 0], ph_recv.at[n, 0], device_id=(gx, to), device_id_type=MESH,
            ).start()

    def send_two(n):
        wait_bytes(r1.at[n], ph_recv.at[n, 0])
        part = tb[n, pl.ds(pl.multiple_of(gy * 8, 8), 8)] + jnp.sum(r1[n], axis=0)
        out_parts[n][...] = part
        for k in GX_ORDER:
            to = lax.rem(gx + k, NGX)
            pltpu.make_async_remote_copy(
                out_parts[n], in_parts[n].at[k - 1],
                ph_send.at[n, 1], ph_recv.at[n, 1], device_id=(to, gy), device_id_type=MESH,
            ).start()

    def send_three(n):
        wait_bytes(in_parts[n], ph_recv.at[n, 1])
        sums = out_parts[n][...] + jnp.sum(in_parts[n][...], axis=0)
        drop = wd[:, 0:128]
        parent = wd[:, 128:256]
        dens = (sums[:, 0:128] + 0.5) / (sums[:, 128:256] + 1.0)
        rise = dens * drop
        seg = lax.broadcasted_iota(jnp.int32, (8, 128), 0)
        press = jnp.where(seg == 0, parent + rise, rise)
        for above in range(7):
            hit = (seg > above) & (parent == float(above))
            press = press + jnp.where(hit, press[above : above + 1], 0.0)
        answer = jnp.concatenate([press, dens], axis=1)
        x3[n] = answer
        mine = pl.ds(pl.multiple_of(gy * 8, 8), 8)
        r3[n, mine] = answer
        for k in GY_ORDER:
            to = lax.rem(gy + k, NGY)
            pltpu.make_async_remote_copy(
                x3.at[n], r3.at[n, mine],
                ph_send.at[n, 2], ph_recv.at[n, 2], device_id=(gx, to), device_id_type=MESH,
            ).start()
        return press

    def answers(n):
        wait_bytes(r3.at[n, pl.ds(0, 56)], ph_recv.at[n, 2])
        seen = dot2(r[:, 0:64], r3[n])
        press = jnp.sum(lm[...] * seen[:, 0:128], axis=1, keepdims=True)
        dens = jnp.sum(lm[...] * seen[:, 128:256], axis=1, keepdims=True)
        depth = (lax.broadcasted_iota(jnp.int32, (1, NZ), 1).astype(F32) + 0.5) / NZ - 0.5
        hi, lo = split(cf[...] * (press + (0.5 * dens) * depth))
        vhl[:, 0:128] = hi
        vhl[:, 128:256] = lo

    def spread_answers():
        both = jnp.dot(s[...], vhl[...], preferred_element_type=F32)
        wl[...] = both[:, 0:128] + both[:, 128:256]

    def pack_rows(state, rows, fields):
        for f in range(fields):
            for x in range(CX):
                rows[0, f, x : x + 1] = state[f, x, CY - 1 : CY]
                rows[1, f, x : x + 1] = state[f, x, 0:1]

    def plane_copies(start, size, sems):
        return [
            pltpu.make_async_remote_copy(
                st1.at[pl.ds(start, size), x], hx1.at[side, pl.ds(start, size)],
                k_send.at[sems + side], k_recv.at[sems + side],
                device_id=(lax.rem(gx + step, NGX), gy), device_id_type=MESH,
            )
            for side, x, step in ((0, CX - 1, 1), (1, 0, NGX - 1))
        ]

    def halo_copies(n, state, planes, rows_out, rows_in):
        up, down = lax.rem(gx + 1, NGX), lax.rem(gx + NGX - 1, NGX)
        right, left = lax.rem(gy + 1, NGY), lax.rem(gy + NGY - 1, NGY)
        four = (
            (state.at[pl.ds(0, 3), CX - 1], planes.at[0], (up, gy)),
            (state.at[pl.ds(0, 3), 0], planes.at[1], (down, gy)),
            (rows_out.at[0], rows_in.at[0], (gx, right)),
            (rows_out.at[1], rows_in.at[1], (gx, left)),
        )
        return [
            pltpu.make_async_remote_copy(
                src, dst, halo_send.at[n, i], halo_recv.at[n, i], device_id=to, device_id_type=MESH
            )
            for i, (src, dst, to) in enumerate(four)
        ]

    def inner_faces(x, c):
        for y0 in range(0, CY, YB):
            ys = slice(y0, y0 + YB)
            p, m1, m2, m34 = (q[f, x, ys] for f in range(4))
            n = [q[f, x + 1, ys] for f in range(4)]
            flow = side_flux(p, (m1, m2, m34), n[0], n[1:], tx[x, ys])
            acc = []
            for f in range(3):
                acc.append(flow[f] - fx[f, ys])
                fx[f, ys] = flow[f]
            n = [q[f, x, y0 + 1 : y0 + 1 + YB] for f in range(4)]
            flow = side_flux(p, (m1, m2, m34), n[0], n[1:], ty[x, ys])
            for f in range(3):
                fy[f, 8 + y0 : 8 + y0 + YB] = flow[f]
                acc[f] = acc[f] + (flow[f] - fy[f, 7 + y0 : 7 + y0 + YB])
            m4 = m1 * (0.2 * p)
            m3 = m34 - m4
            pn, n1, n2, n3, n4 = (pltpu.roll(v, NZ - 1, 1) for v in (p, m1, m2, m3, m4))
            d, total = p - pn, p + pn
            phi1 = d + (0.001 * total + 0.038)
            phi2 = d + (0.0005 * total + 0.049)
            phi3 = d + (0.003 * total + 0.0015)
            t = tz[x, ys]
            up1 = phi1 > 0.0
            t1 = t * phi1
            flow = (
                t1 * jnp.where(up1, m1, n1),
                (t * phi2) * jnp.where(phi2 > 0.0, m2, n2),
                (t * phi3) * jnp.where(phi3 > 0.0, m3, n3) + t1 * jnp.where(up1, m4, n4),
            )
            for f in range(3):
                acc[f] = acc[f] + (flow[f] - pltpu.roll(flow[f], 1, 1))
            sw, sg = c[1, x, ys], c[2, x, ys]
            stored1 = (0.95 + 0.05 * p) * (1.0 - sw - sg)
            stored2 = (0.98 + 0.02 * p) * sw
            stored3 = (0.2 + 0.8 * p) * sg + (0.2 * p) * stored1
            vol = pv[x, ys]
            pull = p * c0[pl.ds(pl.multiple_of(x * CY + y0, YB), YB)]
            for f, (held, m) in enumerate(((stored1, m1), (stored2, m2), (stored3, m34))):
                base[f, x, ys] = vol * held - mo[f, x, ys] + acc[f] + m * pull

    def put_edge(start, size, f, change):
        hi, lo = split(change)
        eh[start : start + size, f * 128 : (f + 1) * 128] = hi
        el[start : start + size, f * 128 : (f + 1) * 128] = lo

    def plane_faces(planes, edges):
        for side, x in ((0, 0), (1, CX - 1)):
            ph = planes[side, 0]
            h1, h2, h3, h4 = mobilities(ph, planes[side, 1], planes[side, 2])
            there, here = (h1, h2, h3 + h4), [q[f, x, 0:CY] for f in (1, 2, 3)]
            p = q[0, x, 0:CY]
            if side == 0:
                flow = side_flux(ph, there, p, here, txb[0])
            else:
                flow = side_flux(p, here, ph, there, txb[1])
            for f in range(3):
                base[f, x] = base[f, x] - flow[f] if side == 0 else base[f, x] + flow[f]
                if edges:
                    change = ns[f, x] * flow[f] if side == 0 else -ns[f, x] * flow[f]
                    put_edge(side * CY, CY, f, change)

    def row_faces(rows, rows_out, edges):
        row_edges = []
        for side, y in ((0, 0), (1, CY - 1)):
            ph = rows[side, 0]
            h1, h2, h3, h4 = mobilities(ph, rows[side, 1], rows[side, 2])
            own_side = 1 - side
            p = rows_out[own_side, 0]
            m1, m2, m3, m4 = mobilities(p, rows_out[own_side, 1], rows_out[own_side, 2])
            there, here = (h1, h2, h3 + h4), (m1, m2, m3 + m4)
            if side == 0:
                flow = side_flux(ph, there, p, here, tyb[0])
            else:
                flow = side_flux(p, here, ph, there, tyb[1])
            for f in range(3):
                change = -flow[f] if side == 0 else flow[f]
                for x in range(CX):
                    base[f, x, y : y + 1] = base[f, x, y : y + 1] + change[x : x + 1]
                if edges:
                    scale = jnp.concatenate([ns[f, x, y : y + 1] for x in range(CX)], axis=0)
                    row_edges.append((f, -scale * change))
        if edges:
            for f in range(3):
                put_edge(2 * CY, 16, f, jnp.concatenate([v for i, v in row_edges if i == f], axis=0))

    def transmissibility(x, c):
        k = st1[3, x]
        nxt = st1[3, jnp.minimum(x + 1, CX - 1)]
        tx[x] = harmonic(k, nxt) * jnp.where(x < CX - 1, 1.0, 0.0)
        ys = lax.broadcasted_iota(jnp.int32, (CY, NZ), 0)
        zs = lax.broadcasted_iota(jnp.int32, (CY, NZ), 1)
        ty[x] = jnp.where(ys == CY - 1, 0.0, harmonic(k, pltpu.roll(k, CY - 1, 0)))
        tz[x] = jnp.where(zs == NZ - 1, 0.0, 0.1 * harmonic(k, pltpu.roll(k, NZ - 1, 1)))
        return c

    def each_plane(body):
        def step(x, c):
            body(x)
            return c
        lax.fori_loop(0, CX, step, 0)

    def pack_wells_data():
        steps = lax.broadcasted_iota(jnp.int32, (8, 8), 0)
        spots = lax.broadcasted_iota(jnp.int32, (8, 8), 1)
        bottom = jnp.sum(jnp.where(steps == spots, bot_ref[...].reshape(1, 8), 0.0), axis=1, keepdims=True)
        parent = jnp.where(spots == 0, bottom, par_ref[...].astype(F32))
        steps = lax.broadcasted_iota(jnp.int32, (8, 128), 0)
        spots = lax.broadcasted_iota(jnp.int32, (8, 128), 1)
        repeat = jnp.where((spots & 7) == steps, 1.0, 0.0)
        both = exact_dot(jnp.concatenate([drop_ref[...], parent], axis=0), repeat)
        flat = jnp.where((spots >> 3) == steps, both[0:8], 0.0) + jnp.where((spots >> 3) - 8 == steps, both[8:16], 0.0)
        w0[...] = jnp.sum(flat, axis=0, keepdims=True)
        wr[gx, 0:1] = w0[...]

    def send_wells_data():
        for k in GX_ORDER:
            pltpu.make_async_remote_copy(
                w0, wr.at[gx, pl.ds(0, 1)], w_send, w_recv,
                device_id=(lax.rem(gx + k, NGX), gy), device_id_type=MESH,
            ).start()

    def place_wells_data():
        wait_bytes(wr.at[pl.ds(0, NGX - 1), pl.ds(0, 1)], w_recv)
        rows = jnp.concatenate([wr[i, 0:1] for i in range(NGX)], axis=0)
        parts = []
        for i in range(3):
            part = rows.astype(BF16)
            parts.append(part.astype(F32))
            rows = rows - parts[-1]
        spots = lax.broadcasted_iota(jnp.int32, (128, 2048), 1)
        wanted = ((spots >> 10) << 6) + ((spots & 7) << 3) + ((spots >> 7) & 7)
        repeat = jnp.where(lax.broadcasted_iota(jnp.int32, (128, 2048), 0) == wanted, 1.0, 0.0).astype(BF16)
        spread = jnp.dot(jnp.concatenate(parts, axis=0).astype(BF16), repeat, preferred_element_type=F32)
        spread = (spread[0:16] + spread[16:32]) + spread[32:48]
        spots = lax.broadcasted_iota(jnp.int32, (NGX, 2048), 1)
        mine = ((spots & 127) >> 3) == lax.broadcasted_iota(jnp.int32, (NGX, 2048), 0)
        spread = jnp.sum(jnp.where(mine, spread, 0.0), axis=0, keepdims=True)
        for seg in range(8):
            wd[seg : seg + 1, 0:128] = spread[:, seg * 128 : (seg + 1) * 128]
            wd[seg : seg + 1, 128:256] = spread[:, (seg + 8) * 128 : (seg + 9) * 128]

    def column_fields(x):
        here = pl.ds(pl.multiple_of(x * CY, CY), CY)
        fields = [st1[f, x] - ns[f, x] * base[f, x] for f in range(3)]
        fields += [ns[f, x] * q[f + 1, x, 0:CY] for f in range(3)]
        for f, field in enumerate(fields):
            hi, lo = split(field)
            dh[here, f * 128 : (f + 1) * 128] = hi
            dl[here, f * 128 : (f + 1) * 128] = lo

    place = jnp.where(
        lax.broadcasted_iota(jnp.int32, (8, 128), 0) + gx * 8 == lax.broadcasted_iota(jnp.int32, (8, 128), 1),
        1.0, 0.0,
    )
    flip = (((1,), (1,)), ((), ()))

    pack_wells_data()

    for i in range(3):
        loads[i].wait()
    for load in loads[4:]:
        load.start()
    each_plane(lambda x: prep(x, st1, True))
    loads[3].wait()
    seen = jnp.dot(g[...], mlh[...], preferred_element_type=F32) + jnp.dot(
        g[...], mll[...], preferred_element_type=F32
    )
    well_sums(0, seen[:, 0:128], seen[:, 128:256])
    loads[4].wait()
    pl.semaphore_wait(barrier, NGX - 1 + NGY - 1)
    k_copies = [
        pltpu.make_async_remote_copy(
            st1.at[3, x], hk.at[i], k_send.at[i], k_recv.at[i],
            device_id=(lax.rem(gx + step, NGX), gy), device_id_type=MESH,
        )
        for i, (x, step) in enumerate(((CX - 1, 1), (0, NGX - 1)))
    ]
    send_wells_data()
    halo_one = halo_copies(0, st1, hx1, hys1, hy1)
    early = plane_copies(0, 1, 2)
    late = plane_copies(1, 2, 4)
    for copy in k_copies + early:
        copy.start()
    send_one(0)

    pack_rows(st1, hys1, 4)
    for f in range(4):
        q[f, CX] = jnp.zeros((CY + 8, NZ), F32)
        for x in range(CX):
            q[f, x, CY : CY + 8] = jnp.zeros((8, NZ), F32)
    for f in range(3):
        fx[f] = jnp.zeros((CY, NZ), F32)
        fy[f, 0:8] = jnp.zeros((8, NZ), F32)
    each_row = lax.broadcasted_iota(jnp.int32, (128, PD), 0)
    for j in range(CX):
        s[j * 128 : (j + 1) * 128] = jnp.where(col == each_row + 128 * j, 1.0, 0.0).astype(BF16)
    here_t = ct[...]
    for j in range(3):
        same[:, j * 128 : (j + 1) * 128] = jnp.where(
            here_t == col[:, j * 128 : (j + 1) * 128], 1.0, 0.0
        ).astype(BF16)
    edge[:, 0:128] = g[:, 0:128]
    edge[:, 128:256] = g[:, COLS - 128 : COLS]
    spot = jnp.where(lanes < 8, lanes * 128, (lanes - 8) * 128 + 127)
    edge[:, 256:384] = jnp.where((here_t == spot) & (lanes < 16), 1.0, 0.0).astype(BF16)
    eh[256:384] = jnp.zeros((128, 384), BF16)
    el[256:384] = jnp.zeros((128, 384), BF16)
    hi, lo = split(cf[...])
    both = jnp.dot(s[...], jnp.concatenate([hi, lo], axis=1), preferred_element_type=F32)
    c0[...] = both[:, 0:128] + both[:, 128:256]
    lax.fori_loop(0, CX, transmissibility, 0)
    send_two(0)
    for copy in halo_one[2:] + late:
        copy.start()

    for i in range(5, 8):
        loads[i].wait()
    each_plane(lambda x: inner_faces(x, st1))
    each_plane(column_fields)
    place_wells_data()
    gq[...] = jnp.dot(g[...], dh[...], preferred_element_type=F32) + jnp.dot(
        g[...], dl[...], preferred_element_type=F32
    )
    send_three(0)

    for copy in k_copies + early + late + halo_one[2:]:
        copy.wait()
    for side, x, there in ((0, 0, gx > 0), (1, CX - 1, gx < NGX - 1)):
        txb[side] = harmonic(hk[side], st1[3, x]) * jnp.where(there, 1.0, 0.0)
    for side, there in ((0, gy > 0), (1, gy < NGY - 1)):
        tyb[side] = harmonic(hy1[side, 3], hys1[1 - side, 3]) * jnp.where(there, 1.0, 0.0)
    plane_faces(hx1, True)
    row_faces(hy1, hys1, True)
    gq[:, 0:384] = gq[:, 0:384] + (
        jnp.dot(edge[...], eh[...], preferred_element_type=F32)
        + jnp.dot(edge[...], el[...], preferred_element_type=F32)
    )
    answers(0)

    both = jnp.dot(same[...], vhl[...], preferred_element_type=F32)
    level = both[:, 0:128] + both[:, 128:256]
    p, sw, sg = (gq[:, f * 128 : (f + 1) * 128] + gq[:, (f + 3) * 128 : (f + 4) * 128] * level for f in range(3))
    m1, m2, m3, m4 = mobilities(p, sw, sg)
    well_sums(1, 0.8 * m1 + m2 + 0.15 * m3, total_mobility(sw, sg))
    send_one(1)
    spread_answers()

    def update(x):
        here = pl.ds(pl.multiple_of(x * CY, CY), CY)
        for f in range(3):
            first = base[f, x] - q[f + 1, x, 0:CY] * wl[here]
            st2[f, x] = st1[f, x] - ns[f, x] * first
        prep(x, st2, False)

    each_plane(update)
    pack_rows(st2, hys2, 3)
    halo_two = halo_copies(1, st2, hx2, hys2, hy2)
    for f in range(3):
        fx[f] = jnp.zeros((CY, NZ), F32)
    send_two(1)
    for copy in halo_two:
        copy.start()
    each_plane(lambda x: inner_faces(x, st2))
    press = send_three(1)
    press_ref[...] = exact_dot(place, press, flip)
    for copy in halo_two:
        copy.wait()
    plane_faces(hx2, False)
    row_faces(hy2, hys2, False)
    answers(1)
    wait_bytes(wr.at[pl.ds(0, NGX - 1), pl.ds(0, 1)], w_send)
    for n in range(2):
        wait_bytes(r1.at[n], ph_send.at[n, 0])
        wait_bytes(in_parts[n], ph_send.at[n, 1])
        wait_bytes(r3.at[n, pl.ds(0, 56)], ph_send.at[n, 2])


def finish(base, q, s, vhl, press, out, press_out, held, sem):
    copies = [pltpu.make_async_copy(press, press_out, sem.at[CX])]
    copies[0].start()
    for x in range(CX):
        both = jnp.dot(s[x * CY : (x + 1) * CY], vhl[...], preferred_element_type=F32)
        wl = both[:, 0:128] + both[:, 128:256]
        for f in range(3):
            held[f, x] = base[f, x] - q[f + 1, x, 0:CY] * wl
        copies.append(pltpu.make_async_copy(held.at[:, x], out.at[:, x], sem.at[x]))
        copies[-1].start()
    for copy in copies:
        copy.wait()


def shards(
    pressure, water_sat, gas_sat, mass_old, pore_volume, permeability, newton_scale, conn_factor,
    perf_column, perf_owner, perf_well, perf_segment, seg_parent, seg_drop, bottom_press,
):
    vmem = pl.BlockSpec(memory_space=pltpu.VMEM)
    hbm = pl.BlockSpec(memory_space=pltpu.HBM)
    cells = (CX, CY, NZ)
    dma = pltpu.SemaphoreType.DMA
    scratch = [
        pltpu.VMEM((4,) + cells, F32),
        pltpu.VMEM((3,) + cells, F32),
        pltpu.VMEM((PD, NZ), F32),
        pltpu.VMEM(cells, F32),
        pltpu.VMEM((3,) + cells, F32),
        pltpu.VMEM((3,) + cells, F32),
        pltpu.VMEM((2, 3, CY, NZ), F32),
        pltpu.VMEM((2, 3, CY, NZ), F32),
        pltpu.VMEM((2, 4, CX, NZ), F32),
        pltpu.VMEM((2, 3, CX, NZ), F32),
        pltpu.VMEM((2, 4, CX, NZ), F32),
        pltpu.VMEM((2, 3, CX, NZ), F32),
        pltpu.VMEM((2, CY, NZ), F32),
        pltpu.VMEM(cells, F32),
        pltpu.VMEM(cells, F32),
        pltpu.VMEM(cells, F32),
        pltpu.VMEM((2, CY, NZ), F32),
        pltpu.VMEM((2, CX, NZ), F32),
        pltpu.VMEM((3, CY, NZ), F32),
        pltpu.VMEM((3, CY + 8, NZ), F32),
        pltpu.VMEM((COLS, NZ), F32),
        pltpu.VMEM((COLS, NZ), F32),
        pltpu.VMEM((PD, COLS), BF16),
        pltpu.VMEM((64, PD), BF16),
        pltpu.VMEM((PD, 128), BF16),
        pltpu.VMEM((PD, 128), F32),
        pltpu.VMEM((COLS, 256), BF16),
        pltpu.VMEM((COLS, 256), BF16),
        pltpu.VMEM((PD, PD), BF16),
        pltpu.VMEM((PD, 128), jnp.int32),
        pltpu.VMEM((PD, 384), BF16),
        pltpu.VMEM((COLS, 768), BF16),
        pltpu.VMEM((COLS, 768), BF16),
        pltpu.VMEM((PD, 768), F32),
        pltpu.VMEM((384, 384), BF16),
        pltpu.VMEM((384, 384), BF16),
        pltpu.VMEM((2, 64, 256), F32),
        pltpu.VMEM((2, NGY - 1, 8, 256), F32),
        pltpu.VMEM((8, 256), F32),
        pltpu.VMEM((NGX - 1, 8, 256), F32),
        pltpu.VMEM((8, 256), F32),
        pltpu.VMEM((NGX - 1, 8, 256), F32),
        pltpu.VMEM((2, 8, 256), F32),
        pltpu.VMEM((2, 64, 256), F32),
        pltpu.VMEM((1, 128), F32),
        pltpu.VMEM((NGX, 8, 128), F32),
        pltpu.VMEM((8, 256), F32),
        pltpu.VMEM((PD,), jnp.int32),
        pltpu.VMEM((1, PD), jnp.int32),
        pltpu.VMEM((PD,), jnp.int32),
        pltpu.VMEM((PD,), jnp.int32),
        pltpu.VMEM((8, 8), jnp.int32),
        pltpu.VMEM((8, 8), F32),
        pltpu.VMEM((8,), F32),
        dma((7,)), dma((8,)), dma((2, 4)), dma((2, 4)), dma((6,)), dma((6,)), dma, dma, dma((2, 3)), dma((2, 3)),
    ]
    fields = (
        pressure, water_sat, gas_sat, mass_old, pore_volume, permeability, newton_scale, conn_factor,
        perf_column, perf_owner.reshape(1, PD), perf_well, perf_segment, seg_parent, seg_drop, bottom_press,
    )
    results = pl.pallas_call(
        kernel,
        out_shape=(
            pltpu.VMEM((3,) + cells, F32),
            pltpu.VMEM((4, CX + 1, CY + 8, NZ), F32),
            pltpu.VMEM((COLS, PD), BF16),
            pltpu.VMEM((PD, 256), BF16),
            pltpu.VMEM((8, 8), F32),
        ),
        in_specs=[hbm] * 15,
        out_specs=(vmem,) * 5,
        scratch_shapes=scratch,
        compiler_params=pltpu.CompilerParams(
            collective_id=0, has_side_effects=True, vmem_limit_bytes=40 << 20
        ),
    )(*[pltpu.with_memory_space_constraint(v, pltpu.HBM) for v in fields])
    return pl.pallas_call(
        finish,
        out_shape=(jax.ShapeDtypeStruct((3,) + cells, F32), jax.ShapeDtypeStruct((8, 8), F32)),
        in_specs=[vmem] * 5,
        out_specs=(hbm, hbm),
        scratch_shapes=[pltpu.VMEM((3,) + cells, F32), dma((CX + 1,))],
        compiler_params=pltpu.CompilerParams(vmem_limit_bytes=6 << 20),
    )(*[pltpu.with_memory_space_constraint(v, pltpu.VMEM) for v in results])


def solution(mesh):
    cell = P("gx", "gy", None)
    triple = P(None, "gx", "gy", None)
    flat = P(("gx", "gy"))
    rows = P(("gx", "gy"), None)
    return jax.shard_map(
        shards,
        mesh=mesh,
        in_specs=(
            cell, cell, cell, triple, cell, cell, triple,
            rows, flat, rows, flat, flat, rows, rows, flat,
        ),
        out_specs=(triple, rows),
        check_vma=False,
    )
```

```python
import functools

import jax
import jax.numpy as jnp
from jax import lax
from jax.experimental import pallas as pl
from jax.experimental.pallas import tpu as pltpu
from jax.sharding import PartitionSpec as P

MESH = pl.DeviceIdType.MESH
F32 = jnp.float32
BF16 = jnp.bfloat16
NGX, NGY = 16, 8
CX, CY, NZ = 8, 128, 128
PD = 384
COLS = CX * CY
YB = 32
GX_ORDER = (10, 9, 11, 6, 14, 2, 8, 5, 7, 13, 15, 1, 3, 4, 12)
GY_ORDER = (4, 3, 5, 2, 6, 1, 7)


def split(v):
    hi = v.astype(BF16)
    return hi, (v - hi.astype(F32)).astype(BF16)


def dot2(one_hot, v):
    hi, lo = split(v)
    return jnp.dot(one_hot, hi, preferred_element_type=F32) + jnp.dot(
        one_hot, lo, preferred_element_type=F32
    )


def exact_dot(a, b, dims=(((1,), (0,)), ((), ()))):
    return lax.dot_general(a, b, dims, precision=lax.Precision.HIGHEST, preferred_element_type=F32)


def mobilities(p, sw, sg):
    so = 1.0 - sw - sg
    m1 = (0.5 * so * so) * (0.95 + 0.05 * p)
    m2 = (2.0 * sw * sw) * (0.98 + 0.02 * p)
    m3 = (5.0 * sg * sg) * (0.2 + 0.8 * p)
    m4 = m1 * (0.2 * p)
    return m1, m2, m3, m4


def total_mobility(sw, sg):
    so = 1.0 - sw - sg
    return 0.5 * so * so + 2.0 * sw * sw + 5.0 * sg * sg


def side_flux(p_i, m_i, p_j, m_j, trans):
    d = p_i - p_j
    up = d > 0.0
    t = trans * d
    return [t * jnp.where(up, a, b) for a, b in zip(m_i, m_j)]


def harmonic(a, b):
    return 2.0 * a * b / (a + b)


def kernel(
    p_h, sw_h, sg_h, mo_h, pv_h, k_h, ns_h, cf_h,
    col_h, own_h, well_h, seg_h, par_h, drop_h, bot_h,
    base, q, s, vhl, press_ref,
    st1, st2, cf, pv, mo, ns, hx1, hx2, hy1, hy2, hys1, hys2,
    hk, tx, ty, tz, txb, tyb, fx, fy, c0, wl,
    g, a_t, r, lm, mlh, mll, same, ct, edge, dh, dl, gq, eh, el,
    tb, r1, x1, r2, y1, r4, x3, r3, w0, wr, wd,
    col_ref, own_ref, well_ref, seg_ref, par_ref, drop_ref, bot_ref,
    small_sem, load_sem, halo_send, halo_recv, k_send, k_recv, w_send, w_recv, ph_send, ph_recv,
):
    gx = lax.axis_index("gx")
    gy = lax.axis_index("gy")

    small = [
        pltpu.make_async_copy(src, dst, small_sem.at[i])
        for i, (src, dst) in enumerate((
            (col_h, col_ref), (own_h, own_ref), (well_h, well_ref), (seg_h, seg_ref),
            (par_h, par_ref), (drop_h, drop_ref), (bot_h, bot_ref),
        ))
    ]
    for load in small:
        load.start()
    loads = [
        pltpu.make_async_copy(p_h, st1.at[0], load_sem.at[0]),
        pltpu.make_async_copy(sw_h, st1.at[1], load_sem.at[1]),
        pltpu.make_async_copy(sg_h, st1.at[2], load_sem.at[2]),
        pltpu.make_async_copy(cf_h, cf, load_sem.at[3]),
        pltpu.make_async_copy(k_h, st1.at[3], load_sem.at[4]),
        pltpu.make_async_copy(pv_h, pv, load_sem.at[5]),
        pltpu.make_async_copy(mo_h, mo, load_sem.at[6]),
        pltpu.make_async_copy(ns_h, ns, load_sem.at[7]),
    ]
    for load in loads[:5]:
        load.start()

    barrier = pltpu.get_barrier_semaphore()
    for k in GX_ORDER:
        pl.semaphore_signal(barrier, 1, device_id=(lax.rem(gx + k, NGX), gy), device_id_type=MESH)
    for k in GY_ORDER:
        pl.semaphore_signal(barrier, 1, device_id=(gx, lax.rem(gy + k, NGY)), device_id_type=MESH)

    for load in small:
        load.wait()
    col = col_ref[...].reshape(1, PD)
    own = own_ref[...]
    row = lax.rem(own, NGY) * 8 + seg_ref[...].reshape(1, PD)
    lane = (own // NGY) * 8 + well_ref[...].reshape(1, PD)
    packed = (col + 1024 * row + 65536 * lane).astype(F32)
    packed_t = jnp.transpose(jnp.broadcast_to(packed, (128, PD))).astype(jnp.int32)
    col_t = packed_t & 1023
    row_t = (packed_t >> 10) & 63
    lane_t = packed_t >> 16
    lanes = lax.broadcasted_iota(jnp.int32, (PD, 128), 1)
    ct[...] = col_t
    lm[...] = jnp.where(lane_t == lanes, 1.0, 0.0)
    r[...] = jnp.where(row_t == lanes, 1.0, 0.0).astype(BF16)
    for j in range(CX):
        g[:, j * 128 : (j + 1) * 128] = jnp.where(col_t == lanes + 128 * j, 1.0, 0.0).astype(BF16)
    rows64 = lax.broadcasted_iota(jnp.int32, (64, PD), 0)
    a_t[...] = jnp.where(row == rows64, 1.0, 0.0).astype(BF16)

    def prep(x, state, sums):
        p, sw, sg = state[0, x], state[1, x], state[2, x]
        m1, m2, m3, m4 = mobilities(p, sw, sg)
        q[0, x, 0:CY] = p
        q[1, x, 0:CY] = m1
        q[2, x, 0:CY] = m2
        q[3, x, 0:CY] = m3 + m4
        if not sums:
            return
        here = pl.ds(pl.multiple_of(x * CY, CY), CY)
        mixed = 0.8 * m1 + m2 + 0.15 * m3
        hi, lo = split(mixed)
        mlh[here, 0:128] = hi
        mll[here, 0:128] = lo
        hi, lo = split(total_mobility(sw, sg))
        mlh[here, 128:256] = hi
        mll[here, 128:256] = lo

    def well_sums(n, mixed, total):
        num = jnp.sum(cf[...] * mixed, axis=1, keepdims=True)
        den = jnp.sum(cf[...] * total, axis=1, keepdims=True)
        spread = jnp.concatenate([lm[...] * num, lm[...] * den], axis=1)
        tb[n] = dot2(a_t[...], spread)

    def wait_bytes(ref, sem):
        pltpu.make_async_copy(ref, ref, sem).wait()

    out_parts = (x1, y1)
    in_parts = (r2, r4)

    def send_one(n):
        for k in GY_ORDER:
            to = lax.rem(gy + k, NGY)
            pltpu.make_async_remote_copy(
                tb.at[n, pl.ds(pl.multiple_of(to * 8, 8), 8)], r1.at[n, k - 1],
                ph_send.at[n, 0], ph_recv.at[n, 0], device_id=(gx, to), device_id_type=MESH,
            ).start()

    def send_two(n):
        wait_bytes(r1.at[n], ph_recv.at[n, 0])
        part = tb[n, pl.ds(pl.multiple_of(gy * 8, 8), 8)] + jnp.sum(r1[n], axis=0)
        out_parts[n][...] = part
        for k in GX_ORDER:
            to = lax.rem(gx + k, NGX)
            pltpu.make_async_remote_copy(
                out_parts[n], in_parts[n].at[k - 1],
                ph_send.at[n, 1], ph_recv.at[n, 1], device_id=(to, gy), device_id_type=MESH,
            ).start()

    def send_three(n):
        wait_bytes(in_parts[n], ph_recv.at[n, 1])
        sums = out_parts[n][...] + jnp.sum(in_parts[n][...], axis=0)
        drop = wd[:, 0:128]
        parent = wd[:, 128:256]
        dens = (sums[:, 0:128] + 0.5) / (sums[:, 128:256] + 1.0)
        rise = dens * drop
        seg = lax.broadcasted_iota(jnp.int32, (8, 128), 0)
        press = jnp.where(seg == 0, parent + rise, rise)
        for above in range(7):
            hit = (seg > above) & (parent == float(above))
            press = press + jnp.where(hit, press[above : above + 1], 0.0)
        answer = jnp.concatenate([press, dens], axis=1)
        x3[n] = answer
        mine = pl.ds(pl.multiple_of(gy * 8, 8), 8)
        r3[n, mine] = answer
        for k in GY_ORDER:
            to = lax.rem(gy + k, NGY)
            pltpu.make_async_remote_copy(
                x3.at[n], r3.at[n, mine],
                ph_send.at[n, 2], ph_recv.at[n, 2], device_id=(gx, to), device_id_type=MESH,
            ).start()
        return press

    def answers(n):
        wait_bytes(r3.at[n, pl.ds(0, 56)], ph_recv.at[n, 2])
        seen = dot2(r[:, 0:64], r3[n])
        press = jnp.sum(lm[...] * seen[:, 0:128], axis=1, keepdims=True)
        dens = jnp.sum(lm[...] * seen[:, 128:256], axis=1, keepdims=True)
        depth = (lax.broadcasted_iota(jnp.int32, (1, NZ), 1).astype(F32) + 0.5) / NZ - 0.5
        hi, lo = split(cf[...] * (press + (0.5 * dens) * depth))
        vhl[:, 0:128] = hi
        vhl[:, 128:256] = lo

    def spread_answers():
        both = jnp.dot(s[...], vhl[...], preferred_element_type=F32)
        wl[...] = both[:, 0:128] + both[:, 128:256]

    def pack_rows(state, rows, fields):
        for f in range(fields):
            for x in range(CX):
                rows[0, f, x : x + 1] = state[f, x, CY - 1 : CY]
                rows[1, f, x : x + 1] = state[f, x, 0:1]

    def plane_copies(start, size, sems):
        return [
            pltpu.make_async_remote_copy(
                st1.at[pl.ds(start, size), x], hx1.at[side, pl.ds(start, size)],
                k_send.at[sems + side], k_recv.at[sems + side],
                device_id=(lax.rem(gx + step, NGX), gy), device_id_type=MESH,
            )
            for side, x, step in ((0, CX - 1, 1), (1, 0, NGX - 1))
        ]

    def halo_copies(n, state, planes, rows_out, rows_in):
        up, down = lax.rem(gx + 1, NGX), lax.rem(gx + NGX - 1, NGX)
        right, left = lax.rem(gy + 1, NGY), lax.rem(gy + NGY - 1, NGY)
        four = (
            (state.at[pl.ds(0, 3), CX - 1], planes.at[0], (up, gy)),
            (state.at[pl.ds(0, 3), 0], planes.at[1], (down, gy)),
            (rows_out.at[0], rows_in.at[0], (gx, right)),
            (rows_out.at[1], rows_in.at[1], (gx, left)),
        )
        return [
            pltpu.make_async_remote_copy(
                src, dst, halo_send.at[n, i], halo_recv.at[n, i], device_id=to, device_id_type=MESH
            )
            for i, (src, dst, to) in enumerate(four)
        ]

    def inner_faces(x, c):
        for y0 in range(0, CY, YB):
            ys = slice(y0, y0 + YB)
            p, m1, m2, m34 = (q[f, x, ys] for f in range(4))
            n = [q[f, x + 1, ys] for f in range(4)]
            flow = side_flux(p, (m1, m2, m34), n[0], n[1:], tx[x, ys])
            acc = []
            for f in range(3):
                acc.append(flow[f] - fx[f, ys])
                fx[f, ys] = flow[f]
            n = [q[f, x, y0 + 1 : y0 + 1 + YB] for f in range(4)]
            flow = side_flux(p, (m1, m2, m34), n[0], n[1:], ty[x, ys])
            for f in range(3):
                fy[f, 8 + y0 : 8 + y0 + YB] = flow[f]
                acc[f] = acc[f] + (flow[f] - fy[f, 7 + y0 : 7 + y0 + YB])
            m4 = m1 * (0.2 * p)
            m3 = m34 - m4
            pn, n1, n2, n3, n4 = (pltpu.roll(v, NZ - 1, 1) for v in (p, m1, m2, m3, m4))
            d, total = p - pn, p + pn
            phi1 = d + (0.001 * total + 0.038)
            phi2 = d + (0.0005 * total + 0.049)
            phi3 = d + (0.003 * total + 0.0015)
            t = tz[x, ys]
            up1 = phi1 > 0.0
            t1 = t * phi1
            flow = (
                t1 * jnp.where(up1, m1, n1),
                (t * phi2) * jnp.where(phi2 > 0.0, m2, n2),
                (t * phi3) * jnp.where(phi3 > 0.0, m3, n3) + t1 * jnp.where(up1, m4, n4),
            )
            for f in range(3):
                acc[f] = acc[f] + (flow[f] - pltpu.roll(flow[f], 1, 1))
            sw, sg = c[1, x, ys], c[2, x, ys]
            stored1 = (0.95 + 0.05 * p) * (1.0 - sw - sg)
            stored2 = (0.98 + 0.02 * p) * sw
            stored3 = (0.2 + 0.8 * p) * sg + (0.2 * p) * stored1
            vol = pv[x, ys]
            pull = p * c0[pl.ds(pl.multiple_of(x * CY + y0, YB), YB)]
            for f, (held, m) in enumerate(((stored1, m1), (stored2, m2), (stored3, m34))):
                base[f, x, ys] = vol * held - mo[f, x, ys] + acc[f] + m * pull

    def put_edge(start, size, f, change):
        hi, lo = split(change)
        eh[start : start + size, f * 128 : (f + 1) * 128] = hi
        el[start : start + size, f * 128 : (f + 1) * 128] = lo

    def plane_faces(planes, edges):
        for side, x in ((0, 0), (1, CX - 1)):
            ph = planes[side, 0]
            h1, h2, h3, h4 = mobilities(ph, planes[side, 1], planes[side, 2])
            there, here = (h1, h2, h3 + h4), [q[f, x, 0:CY] for f in (1, 2, 3)]
            p = q[0, x, 0:CY]
            if side == 0:
                flow = side_flux(ph, there, p, here, txb[0])
            else:
                flow = side_flux(p, here, ph, there, txb[1])
            for f in range(3):
                base[f, x] = base[f, x] - flow[f] if side == 0 else base[f, x] + flow[f]
                if edges:
                    change = ns[f, x] * flow[f] if side == 0 else -ns[f, x] * flow[f]
                    put_edge(side * CY, CY, f, change)

    def row_faces(rows, rows_out, edges):
        row_edges = []
        for side, y in ((0, 0), (1, CY - 1)):
            ph = rows[side, 0]
            h1, h2, h3, h4 = mobilities(ph, rows[side, 1], rows[side, 2])
            own_side = 1 - side
            p = rows_out[own_side, 0]
            m1, m2, m3, m4 = mobilities(p, rows_out[own_side, 1], rows_out[own_side, 2])
            there, here = (h1, h2, h3 + h4), (m1, m2, m3 + m4)
            if side == 0:
                flow = side_flux(ph, there, p, here, tyb[0])
            else:
                flow = side_flux(p, here, ph, there, tyb[1])
            for f in range(3):
                change = -flow[f] if side == 0 else flow[f]
                for x in range(CX):
                    base[f, x, y : y + 1] = base[f, x, y : y + 1] + change[x : x + 1]
                if edges:
                    scale = jnp.concatenate([ns[f, x, y : y + 1] for x in range(CX)], axis=0)
                    row_edges.append((f, -scale * change))
        if edges:
            for f in range(3):
                put_edge(2 * CY, 16, f, jnp.concatenate([v for i, v in row_edges if i == f], axis=0))

    def transmissibility(x, c):
        k = st1[3, x]
        nxt = st1[3, jnp.minimum(x + 1, CX - 1)]
        tx[x] = harmonic(k, nxt) * jnp.where(x < CX - 1, 1.0, 0.0)
        ys = lax.broadcasted_iota(jnp.int32, (CY, NZ), 0)
        zs = lax.broadcasted_iota(jnp.int32, (CY, NZ), 1)
        ty[x] = jnp.where(ys == CY - 1, 0.0, harmonic(k, pltpu.roll(k, CY - 1, 0)))
        tz[x] = jnp.where(zs == NZ - 1, 0.0, 0.1 * harmonic(k, pltpu.roll(k, NZ - 1, 1)))
        return c

    def each_plane(body, first=0, last=CX):
        def step(x, c):
            body(x)
            return c
        lax.fori_loop(first, last, step, 0)

    def pack_wells_data():
        steps = lax.broadcasted_iota(jnp.int32, (8, 8), 0)
        spots = lax.broadcasted_iota(jnp.int32, (8, 8), 1)
        bottom = jnp.sum(jnp.where(steps == spots, bot_ref[...].reshape(1, 8), 0.0), axis=1, keepdims=True)
        parent = jnp.where(spots == 0, bottom, par_ref[...].astype(F32))
        steps = lax.broadcasted_iota(jnp.int32, (8, 128), 0)
        spots = lax.broadcasted_iota(jnp.int32, (8, 128), 1)
        repeat = jnp.where((spots & 7) == steps, 1.0, 0.0)
        both = exact_dot(jnp.concatenate([drop_ref[...], parent], axis=0), repeat)
        flat = jnp.where((spots >> 3) == steps, both[0:8], 0.0) + jnp.where((spots >> 3) - 8 == steps, both[8:16], 0.0)
        w0[...] = jnp.sum(flat, axis=0, keepdims=True)
        wr[gx, 0:1] = w0[...]

    def send_wells_data():
        for k in GX_ORDER:
            pltpu.make_async_remote_copy(
                w0, wr.at[gx, pl.ds(0, 1)], w_send, w_recv,
                device_id=(lax.rem(gx + k, NGX), gy), device_id_type=MESH,
            ).start()

    def place_wells_data():
        wait_bytes(wr.at[pl.ds(0, NGX - 1), pl.ds(0, 1)], w_recv)
        rows = jnp.concatenate([wr[i, 0:1] for i in range(NGX)], axis=0)
        parts = []
        for i in range(3):
            part = rows.astype(BF16)
            parts.append(part.astype(F32))
            rows = rows - parts[-1]
        spots = lax.broadcasted_iota(jnp.int32, (128, 2048), 1)
        wanted = ((spots >> 10) << 6) + ((spots & 7) << 3) + ((spots >> 7) & 7)
        repeat = jnp.where(lax.broadcasted_iota(jnp.int32, (128, 2048), 0) == wanted, 1.0, 0.0).astype(BF16)
        spread = jnp.dot(jnp.concatenate(parts, axis=0).astype(BF16), repeat, preferred_element_type=F32)
        spread = (spread[0:16] + spread[16:32]) + spread[32:48]
        spots = lax.broadcasted_iota(jnp.int32, (NGX, 2048), 1)
        mine = ((spots & 127) >> 3) == lax.broadcasted_iota(jnp.int32, (NGX, 2048), 0)
        spread = jnp.sum(jnp.where(mine, spread, 0.0), axis=0, keepdims=True)
        for seg in range(8):
            wd[seg : seg + 1, 0:128] = spread[:, seg * 128 : (seg + 1) * 128]
            wd[seg : seg + 1, 128:256] = spread[:, (seg + 8) * 128 : (seg + 9) * 128]

    def column_fields(x):
        here = pl.ds(pl.multiple_of(x * CY, CY), CY)
        fields = [st1[f, x] - ns[f, x] * base[f, x] for f in range(3)]
        fields += [ns[f, x] * q[f + 1, x, 0:CY] for f in range(3)]
        for f, field in enumerate(fields):
            hi, lo = split(field)
            dh[here, f * 128 : (f + 1) * 128] = hi
            dl[here, f * 128 : (f + 1) * 128] = lo

    place = jnp.where(
        lax.broadcasted_iota(jnp.int32, (8, 128), 0) + gx * 8 == lax.broadcasted_iota(jnp.int32, (8, 128), 1),
        1.0, 0.0,
    )
    flip = (((1,), (1,)), ((), ()))

    pack_wells_data()

    for i in range(3):
        loads[i].wait()
    for load in loads[5:]:
        load.start()
    each_plane(lambda x: prep(x, st1, True))
    loads[3].wait()
    seen = jnp.dot(g[...], mlh[...], preferred_element_type=F32) + jnp.dot(
        g[...], mll[...], preferred_element_type=F32
    )
    well_sums(0, seen[:, 0:128], seen[:, 128:256])
    loads[4].wait()
    pl.semaphore_wait(barrier, NGX - 1 + NGY - 1)
    k_copies = [
        pltpu.make_async_remote_copy(
            st1.at[3, x], hk.at[i], k_send.at[i], k_recv.at[i],
            device_id=(lax.rem(gx + step, NGX), gy), device_id_type=MESH,
        )
        for i, (x, step) in enumerate(((CX - 1, 1), (0, NGX - 1)))
    ]
    send_wells_data()
    halo_one = halo_copies(0, st1, hx1, hys1, hy1)
    early = plane_copies(0, 1, 2)
    late = plane_copies(1, 2, 4)
    for copy in k_copies + early:
        copy.start()
    send_one(0)

    pack_rows(st1, hys1, 4)
    for f in range(4):
        q[f, CX] = jnp.zeros((CY + 8, NZ), F32)
        for x in range(CX):
            q[f, x, CY : CY + 8] = jnp.zeros((8, NZ), F32)
    for f in range(3):
        fx[f] = jnp.zeros((CY, NZ), F32)
        fy[f, 0:8] = jnp.zeros((8, NZ), F32)
    each_row = lax.broadcasted_iota(jnp.int32, (128, PD), 0)
    for j in range(CX):
        s[j * 128 : (j + 1) * 128] = jnp.where(col == each_row + 128 * j, 1.0, 0.0).astype(BF16)
    here_t = ct[...]
    for j in range(3):
        same[:, j * 128 : (j + 1) * 128] = jnp.where(
            here_t == col[:, j * 128 : (j + 1) * 128], 1.0, 0.0
        ).astype(BF16)
    edge[:, 0:128] = g[:, 0:128]
    edge[:, 128:256] = g[:, COLS - 128 : COLS]
    spot = jnp.where(lanes < 8, lanes * 128, (lanes - 8) * 128 + 127)
    edge[:, 256:384] = jnp.where((here_t == spot) & (lanes < 16), 1.0, 0.0).astype(BF16)
    eh[256:384] = jnp.zeros((128, 384), BF16)
    el[256:384] = jnp.zeros((128, 384), BF16)
    hi, lo = split(cf[...])
    both = jnp.dot(s[...], jnp.concatenate([hi, lo], axis=1), preferred_element_type=F32)
    c0[...] = both[:, 0:128] + both[:, 128:256]
    lax.fori_loop(0, CX, transmissibility, 0)
    send_two(0)
    for copy in halo_one[2:] + late:
        copy.start()

    for i in range(5, 8):
        loads[i].wait()
    each_plane(lambda x: inner_faces(x, st1))
    each_plane(column_fields)
    place_wells_data()
    gq[...] = jnp.dot(g[...], dh[...], preferred_element_type=F32) + jnp.dot(
        g[...], dl[...], preferred_element_type=F32
    )
    send_three(0)

    for copy in k_copies + early + late + halo_one[2:]:
        copy.wait()
    for side, x, there in ((0, 0, gx > 0), (1, CX - 1, gx < NGX - 1)):
        txb[side] = harmonic(hk[side], st1[3, x]) * jnp.where(there, 1.0, 0.0)
    for side, there in ((0, gy > 0), (1, gy < NGY - 1)):
        tyb[side] = harmonic(hy1[side, 3], hys1[1 - side, 3]) * jnp.where(there, 1.0, 0.0)
    plane_faces(hx1, True)
    row_faces(hy1, hys1, True)
    gq[:, 0:384] = gq[:, 0:384] + (
        jnp.dot(edge[...], eh[...], preferred_element_type=F32)
        + jnp.dot(edge[...], el[...], preferred_element_type=F32)
    )
    answers(0)

    both = jnp.dot(same[...], vhl[...], preferred_element_type=F32)
    level = both[:, 0:128] + both[:, 128:256]
    p, sw, sg = (gq[:, f * 128 : (f + 1) * 128] + gq[:, (f + 3) * 128 : (f + 4) * 128] * level for f in range(3))
    m1, m2, m3, m4 = mobilities(p, sw, sg)
    well_sums(1, 0.8 * m1 + m2 + 0.15 * m3, total_mobility(sw, sg))
    send_one(1)
    spread_answers()

    def update(x):
        here = pl.ds(pl.multiple_of(x * CY, CY), CY)
        for f in range(3):
            first = base[f, x] - q[f + 1, x, 0:CY] * wl[here]
            st2[f, x] = st1[f, x] - ns[f, x] * first
        prep(x, st2, False)

    each_plane(update)
    pack_rows(st2, hys2, 3)
    halo_two = halo_copies(1, st2, hx2, hys2, hy2)
    for f in range(3):
        fx[f] = jnp.zeros((CY, NZ), F32)
    send_two(1)
    each_plane(lambda x: inner_faces(x, st2), 0, 5)
    for copy in halo_two:
        copy.start()
    each_plane(lambda x: inner_faces(x, st2), 5, CX)
    press = send_three(1)
    press_ref[...] = exact_dot(place, press, flip)
    for copy in halo_two:
        copy.wait()
    plane_faces(hx2, False)
    row_faces(hy2, hys2, False)
    answers(1)
    wait_bytes(wr.at[pl.ds(0, NGX - 1), pl.ds(0, 1)], w_send)
    for n in range(2):
        wait_bytes(r1.at[n], ph_send.at[n, 0])
        wait_bytes(in_parts[n], ph_send.at[n, 1])
        wait_bytes(r3.at[n, pl.ds(0, 56)], ph_send.at[n, 2])


def finish(base, q, s, vhl, press, out, press_out, held, sem):
    copies = [pltpu.make_async_copy(press, press_out, sem.at[CX])]
    copies[0].start()
    for start in range(0, CX, 2):
        both = jnp.dot(s[start * CY : (start + 2) * CY], vhl[...], preferred_element_type=F32)
        for x in range(start, start + 2):
            here = slice((x - start) * CY, (x - start + 1) * CY)
            wl = both[here, 0:128] + both[here, 128:256]
            for f in range(3):
                held[f, x] = base[f, x] - q[f + 1, x, 0:CY] * wl
            copies.append(pltpu.make_async_copy(held.at[:, x], out.at[:, x], sem.at[x]))
            copies[-1].start()
    for copy in copies:
        copy.wait()


def shards(
    pressure, water_sat, gas_sat, mass_old, pore_volume, permeability, newton_scale, conn_factor,
    perf_column, perf_owner, perf_well, perf_segment, seg_parent, seg_drop, bottom_press,
):
    vmem = pl.BlockSpec(memory_space=pltpu.VMEM)
    hbm = pl.BlockSpec(memory_space=pltpu.HBM)
    cells = (CX, CY, NZ)
    dma = pltpu.SemaphoreType.DMA
    scratch = [
        pltpu.VMEM((4,) + cells, F32),
        pltpu.VMEM((3,) + cells, F32),
        pltpu.VMEM((PD, NZ), F32),
        pltpu.VMEM(cells, F32),
        pltpu.VMEM((3,) + cells, F32),
        pltpu.VMEM((3,) + cells, F32),
        pltpu.VMEM((2, 3, CY, NZ), F32),
        pltpu.VMEM((2, 3, CY, NZ), F32),
        pltpu.VMEM((2, 4, CX, NZ), F32),
        pltpu.VMEM((2, 3, CX, NZ), F32),
        pltpu.VMEM((2, 4, CX, NZ), F32),
        pltpu.VMEM((2, 3, CX, NZ), F32),
        pltpu.VMEM((2, CY, NZ), F32),
        pltpu.VMEM(cells, F32),
        pltpu.VMEM(cells, F32),
        pltpu.VMEM(cells, F32),
        pltpu.VMEM((2, CY, NZ), F32),
        pltpu.VMEM((2, CX, NZ), F32),
        pltpu.VMEM((3, CY, NZ), F32),
        pltpu.VMEM((3, CY + 8, NZ), F32),
        pltpu.VMEM((COLS, NZ), F32),
        pltpu.VMEM((COLS, NZ), F32),
        pltpu.VMEM((PD, COLS), BF16),
        pltpu.VMEM((64, PD), BF16),
        pltpu.VMEM((PD, 128), BF16),
        pltpu.VMEM((PD, 128), F32),
        pltpu.VMEM((COLS, 256), BF16),
        pltpu.VMEM((COLS, 256), BF16),
        pltpu.VMEM((PD, PD), BF16),
        pltpu.VMEM((PD, 128), jnp.int32),
        pltpu.VMEM((PD, 384), BF16),
        pltpu.VMEM((COLS, 768), BF16),
        pltpu.VMEM((COLS, 768), BF16),
        pltpu.VMEM((PD, 768), F32),
        pltpu.VMEM((384, 384), BF16),
        pltpu.VMEM((384, 384), BF16),
        pltpu.VMEM((2, 64, 256), F32),
        pltpu.VMEM((2, NGY - 1, 8, 256), F32),
        pltpu.VMEM((8, 256), F32),
        pltpu.VMEM((NGX - 1, 8, 256), F32),
        pltpu.VMEM((8, 256), F32),
        pltpu.VMEM((NGX - 1, 8, 256), F32),
        pltpu.VMEM((2, 8, 256), F32),
        pltpu.VMEM((2, 64, 256), F32),
        pltpu.VMEM((1, 128), F32),
        pltpu.VMEM((NGX, 8, 128), F32),
        pltpu.VMEM((8, 256), F32),
        pltpu.VMEM((PD,), jnp.int32),
        pltpu.VMEM((1, PD), jnp.int32),
        pltpu.VMEM((PD,), jnp.int32),
        pltpu.VMEM((PD,), jnp.int32),
        pltpu.VMEM((8, 8), jnp.int32),
        pltpu.VMEM((8, 8), F32),
        pltpu.VMEM((8,), F32),
        dma((7,)), dma((8,)), dma((2, 4)), dma((2, 4)), dma((6,)), dma((6,)), dma, dma, dma((2, 3)), dma((2, 3)),
    ]
    fields = (
        pressure, water_sat, gas_sat, mass_old, pore_volume, permeability, newton_scale, conn_factor,
        perf_column, perf_owner.reshape(1, PD), perf_well, perf_segment, seg_parent, seg_drop, bottom_press,
    )
    results = pl.pallas_call(
        kernel,
        out_shape=(
            pltpu.VMEM((3,) + cells, F32),
            pltpu.VMEM((4, CX + 1, CY + 8, NZ), F32),
            pltpu.VMEM((COLS, PD), BF16),
            pltpu.VMEM((PD, 256), BF16),
            pltpu.VMEM((8, 8), F32),
        ),
        in_specs=[hbm] * 15,
        out_specs=(vmem,) * 5,
        scratch_shapes=scratch,
        compiler_params=pltpu.CompilerParams(
            collective_id=0, has_side_effects=True, vmem_limit_bytes=40 << 20
        ),
    )(*[pltpu.with_memory_space_constraint(v, pltpu.HBM) for v in fields])
    return pl.pallas_call(
        finish,
        out_shape=(jax.ShapeDtypeStruct((3,) + cells, F32), jax.ShapeDtypeStruct((8, 8), F32)),
        in_specs=[vmem] * 5,
        out_specs=(hbm, hbm),
        scratch_shapes=[pltpu.VMEM((3,) + cells, F32), dma((CX + 1,))],
        compiler_params=pltpu.CompilerParams(vmem_limit_bytes=6 << 20),
    )(*[pltpu.with_memory_space_constraint(v, pltpu.VMEM) for v in results])


def solution(mesh):
    cell = P("gx", "gy", None)
    triple = P(None, "gx", "gy", None)
    flat = P(("gx", "gy"))
    rows = P(("gx", "gy"), None)
    return jax.shard_map(
        shards,
        mesh=mesh,
        in_specs=(
            cell, cell, cell, triple, cell, cell, triple,
            rows, flat, rows, flat, flat, rows, rows, flat,
        ),
        out_specs=(triple, rows),
        check_vma=False,
    )
```

```python
import functools

import jax
import jax.numpy as jnp
from jax import lax
from jax.experimental import pallas as pl
from jax.experimental.pallas import tpu as pltpu
from jax.sharding import PartitionSpec as P

MESH = pl.DeviceIdType.MESH
F32 = jnp.float32
BF16 = jnp.bfloat16
NGX, NGY = 16, 8
CX, CY, NZ = 8, 128, 128
PD = 384
COLS = CX * CY
YB = 32
GX_ORDER = (10, 9, 11, 6, 14, 2, 8, 5, 7, 13, 15, 1, 3, 4, 12)
GY_ORDER = (4, 3, 5, 2, 6, 1, 7)


def split(v):
    hi = v.astype(BF16)
    return hi, (v - hi.astype(F32)).astype(BF16)


def dot2(one_hot, v):
    hi, lo = split(v)
    return jnp.dot(one_hot, hi, preferred_element_type=F32) + jnp.dot(
        one_hot, lo, preferred_element_type=F32
    )


def exact_dot(a, b, dims=(((1,), (0,)), ((), ()))):
    return lax.dot_general(a, b, dims, precision=lax.Precision.HIGHEST, preferred_element_type=F32)


def mobilities(p, sw, sg):
    so = 1.0 - sw - sg
    m1 = (0.5 * so * so) * (0.95 + 0.05 * p)
    m2 = (2.0 * sw * sw) * (0.98 + 0.02 * p)
    m3 = (5.0 * sg * sg) * (0.2 + 0.8 * p)
    m4 = m1 * (0.2 * p)
    return m1, m2, m3, m4


def total_mobility(sw, sg):
    so = 1.0 - sw - sg
    return 0.5 * so * so + 2.0 * sw * sw + 5.0 * sg * sg


def side_flux(p_i, m_i, p_j, m_j, trans):
    d = p_i - p_j
    up = d > 0.0
    t = trans * d
    return [t * jnp.where(up, a, b) for a, b in zip(m_i, m_j)]


def harmonic(a, b):
    return 2.0 * a * b / (a + b)


def kernel(
    p_h, sw_h, sg_h, mo_h, pv_h, k_h, ns_h, cf_h,
    col_h, own_h, well_h, seg_h, par_h, drop_h, bot_h,
    base, q, s, vhl, press_ref,
    st1, st2, cf, pv, mo, ns, hx1, hx2, hy1, hy2, hys1, hys2,
    hk, tx, ty, tz, txb, tyb, fx, fy, c0, wl,
    g, a_t, r, lm, mlh, mll, same, ct, edge, dh, dl, gq, eh, el,
    tb, r1, x1, r2, y1, r4, x3, r3, w0, wr, wd,
    col_ref, own_ref, well_ref, seg_ref, par_ref, drop_ref, bot_ref,
    small_sem, load_sem, halo_send, halo_recv, k_send, k_recv, w_send, w_recv, ph_send, ph_recv,
):
    gx = lax.axis_index("gx")
    gy = lax.axis_index("gy")

    small = [
        pltpu.make_async_copy(src, dst, small_sem.at[i])
        for i, (src, dst) in enumerate((
            (col_h, col_ref), (own_h, own_ref), (well_h, well_ref), (seg_h, seg_ref),
            (par_h, par_ref), (drop_h, drop_ref), (bot_h, bot_ref),
        ))
    ]
    for load in small:
        load.start()
    loads = [
        pltpu.make_async_copy(p_h, st1.at[0], load_sem.at[0]),
        pltpu.make_async_copy(sw_h, st1.at[1], load_sem.at[1]),
        pltpu.make_async_copy(sg_h, st1.at[2], load_sem.at[2]),
        pltpu.make_async_copy(cf_h, cf, load_sem.at[3]),
        pltpu.make_async_copy(k_h, st1.at[3], load_sem.at[4]),
        pltpu.make_async_copy(pv_h, pv, load_sem.at[5]),
        pltpu.make_async_copy(mo_h, mo, load_sem.at[6]),
        pltpu.make_async_copy(ns_h, ns, load_sem.at[7]),
    ]
    for load in loads[:5]:
        load.start()

    barrier = pltpu.get_barrier_semaphore()
    for k in GX_ORDER:
        pl.semaphore_signal(barrier, 1, device_id=(lax.rem(gx + k, NGX), gy), device_id_type=MESH)
    for k in GY_ORDER:
        pl.semaphore_signal(barrier, 1, device_id=(gx, lax.rem(gy + k, NGY)), device_id_type=MESH)

    for load in small:
        load.wait()
    col = col_ref[...].reshape(1, PD)
    own = own_ref[...]
    row = lax.rem(own, NGY) * 8 + seg_ref[...].reshape(1, PD)
    lane = (own // NGY) * 8 + well_ref[...].reshape(1, PD)
    packed = (col + 1024 * row + 65536 * lane).astype(F32)
    packed_t = jnp.transpose(jnp.broadcast_to(packed, (128, PD))).astype(jnp.int32)
    col_t = packed_t & 1023
    row_t = (packed_t >> 10) & 63
    lane_t = packed_t >> 16
    lanes = lax.broadcasted_iota(jnp.int32, (PD, 128), 1)
    ct[...] = col_t
    lm[...] = jnp.where(lane_t == lanes, 1.0, 0.0)
    r[...] = jnp.where(row_t == (lanes & 63), 1.0, 0.0).astype(BF16)
    for j in range(CX):
        g[:, j * 128 : (j + 1) * 128] = jnp.where(col_t == lanes + 128 * j, 1.0, 0.0).astype(BF16)
    rows64 = lax.broadcasted_iota(jnp.int32, (64, PD), 0)
    a_t[...] = jnp.where(row == rows64, 1.0, 0.0).astype(BF16)

    def prep(x, state, sums):
        p, sw, sg = state[0, x], state[1, x], state[2, x]
        m1, m2, m3, m4 = mobilities(p, sw, sg)
        q[0, x, 0:CY] = p
        q[1, x, 0:CY] = m1
        q[2, x, 0:CY] = m2
        q[3, x, 0:CY] = m3 + m4
        if not sums:
            return
        here = pl.ds(pl.multiple_of(x * CY, CY), CY)
        mixed = 0.8 * m1 + m2 + 0.15 * m3
        hi, lo = split(mixed)
        mlh[here, 0:128] = hi
        mll[here, 0:128] = lo
        hi, lo = split(total_mobility(sw, sg))
        mlh[here, 128:256] = hi
        mll[here, 128:256] = lo

    def well_sums(n, mixed, total):
        num = jnp.sum(cf[...] * mixed, axis=1, keepdims=True)
        den = jnp.sum(cf[...] * total, axis=1, keepdims=True)
        spread = jnp.concatenate([lm[...] * num, lm[...] * den], axis=1)
        tb[n] = dot2(a_t[...], spread)

    def wait_bytes(ref, sem):
        pltpu.make_async_copy(ref, ref, sem).wait()

    out_parts = (x1, y1)
    in_parts = (r2, r4)

    def send_one(n):
        for k in GY_ORDER:
            to = lax.rem(gy + k, NGY)
            pltpu.make_async_remote_copy(
                tb.at[n, pl.ds(pl.multiple_of(to * 8, 8), 8)], r1.at[n, k - 1],
                ph_send.at[n, 0], ph_recv.at[n, 0], device_id=(gx, to), device_id_type=MESH,
            ).start()

    def send_two(n):
        wait_bytes(r1.at[n], ph_recv.at[n, 0])
        part = tb[n, pl.ds(pl.multiple_of(gy * 8, 8), 8)] + jnp.sum(r1[n], axis=0)
        out_parts[n][...] = part
        for k in GX_ORDER:
            to = lax.rem(gx + k, NGX)
            pltpu.make_async_remote_copy(
                out_parts[n], in_parts[n].at[k - 1],
                ph_send.at[n, 1], ph_recv.at[n, 1], device_id=(to, gy), device_id_type=MESH,
            ).start()

    def send_three(n):
        wait_bytes(in_parts[n], ph_recv.at[n, 1])
        sums = out_parts[n][...] + jnp.sum(in_parts[n][...], axis=0)
        drop = wd[:, 0:128]
        parent = wd[:, 128:256]
        dens = (sums[:, 0:128] + 0.5) / (sums[:, 128:256] + 1.0)
        rise = dens * drop
        seg = lax.broadcasted_iota(jnp.int32, (8, 128), 0)
        press = jnp.where(seg == 0, parent + rise, rise)
        for above in range(7):
            hit = (seg > above) & (parent == float(above))
            press = press + jnp.where(hit, press[above : above + 1], 0.0)
        answer = jnp.concatenate([press, dens], axis=1)
        x3[n] = answer
        mine = pl.ds(pl.multiple_of(gy * 8, 8), 8)
        r3[n, mine] = answer
        for k in GY_ORDER:
            to = lax.rem(gy + k, NGY)
            pltpu.make_async_remote_copy(
                x3.at[n], r3.at[n, mine],
                ph_send.at[n, 2], ph_recv.at[n, 2], device_id=(gx, to), device_id_type=MESH,
            ).start()
        return press

    def answers(n):
        wait_bytes(r3.at[n, pl.ds(0, 56)], ph_recv.at[n, 2])
        seen = jnp.dot(r[...], jnp.concatenate(split(r3[n]), axis=0), preferred_element_type=F32)
        press = jnp.sum(lm[...] * seen[:, 0:128], axis=1, keepdims=True)
        dens = jnp.sum(lm[...] * seen[:, 128:256], axis=1, keepdims=True)
        depth = (lax.broadcasted_iota(jnp.int32, (1, NZ), 1).astype(F32) + 0.5) / NZ - 0.5
        hi, lo = split(cf[...] * (press + (0.5 * dens) * depth))
        vhl[:, 0:128] = hi
        vhl[:, 128:256] = lo

    def spread_answers():
        both = jnp.dot(s[...], vhl[...], preferred_element_type=F32)
        wl[...] = both[:, 0:128] + both[:, 128:256]

    def pack_rows(state, rows, fields):
        for f in range(fields):
            for x in range(CX):
                rows[0, f, x : x + 1] = state[f, x, CY - 1 : CY]
                rows[1, f, x : x + 1] = state[f, x, 0:1]

    def plane_copies(start, size, sems):
        return [
            pltpu.make_async_remote_copy(
                st1.at[pl.ds(start, size), x], hx1.at[side, pl.ds(start, size)],
                k_send.at[sems + side], k_recv.at[sems + side],
                device_id=(lax.rem(gx + step, NGX), gy), device_id_type=MESH,
            )
            for side, x, step in ((0, CX - 1, 1), (1, 0, NGX - 1))
        ]

    def halo_copies(n, state, planes, rows_out, rows_in):
        up, down = lax.rem(gx + 1, NGX), lax.rem(gx + NGX - 1, NGX)
        right, left = lax.rem(gy + 1, NGY), lax.rem(gy + NGY - 1, NGY)
        four = (
            (state.at[pl.ds(0, 3), CX - 1], planes.at[0], (up, gy)),
            (state.at[pl.ds(0, 3), 0], planes.at[1], (down, gy)),
            (rows_out.at[0], rows_in.at[0], (gx, right)),
            (rows_out.at[1], rows_in.at[1], (gx, left)),
        )
        return [
            pltpu.make_async_remote_copy(
                src, dst, halo_send.at[n, i], halo_recv.at[n, i], device_id=to, device_id_type=MESH
            )
            for i, (src, dst, to) in enumerate(four)
        ]

    def inner_faces(x, c):
        for y0 in range(0, CY, YB):
            ys = slice(y0, y0 + YB)
            p, m1, m2, m34 = (q[f, x, ys] for f in range(4))
            n = [q[f, x + 1, ys] for f in range(4)]
            flow = side_flux(p, (m1, m2, m34), n[0], n[1:], tx[x, ys])
            acc = []
            for f in range(3):
                acc.append(flow[f] - fx[f, ys])
                fx[f, ys] = flow[f]
            n = [q[f, x, y0 + 1 : y0 + 1 + YB] for f in range(4)]
            flow = side_flux(p, (m1, m2, m34), n[0], n[1:], ty[x, ys])
            for f in range(3):
                fy[f, 8 + y0 : 8 + y0 + YB] = flow[f]
                acc[f] = acc[f] + (flow[f] - fy[f, 7 + y0 : 7 + y0 + YB])
            m4 = m1 * (0.2 * p)
            m3 = m34 - m4
            pn, n1, n2, n3, n4 = (pltpu.roll(v, NZ - 1, 1) for v in (p, m1, m2, m3, m4))
            d, total = p - pn, p + pn
            phi1 = d + (0.001 * total + 0.038)
            phi2 = d + (0.0005 * total + 0.049)
            phi3 = d + (0.003 * total + 0.0015)
            t = tz[x, ys]
            up1 = phi1 > 0.0
            t1 = t * phi1
            flow = (
                t1 * jnp.where(up1, m1, n1),
                (t * phi2) * jnp.where(phi2 > 0.0, m2, n2),
                (t * phi3) * jnp.where(phi3 > 0.0, m3, n3) + t1 * jnp.where(up1, m4, n4),
            )
            for f in range(3):
                acc[f] = acc[f] + (flow[f] - pltpu.roll(flow[f], 1, 1))
            sw, sg = c[1, x, ys], c[2, x, ys]
            stored1 = (0.95 + 0.05 * p) * (1.0 - sw - sg)
            stored2 = (0.98 + 0.02 * p) * sw
            stored3 = (0.2 + 0.8 * p) * sg + (0.2 * p) * stored1
            vol = pv[x, ys]
            pull = p * c0[pl.ds(pl.multiple_of(x * CY + y0, YB), YB)]
            for f, (held, m) in enumerate(((stored1, m1), (stored2, m2), (stored3, m34))):
                base[f, x, ys] = vol * held - mo[f, x, ys] + acc[f] + m * pull

    def put_edge(start, size, f, change):
        hi, lo = split(change)
        eh[start : start + size, f * 128 : (f + 1) * 128] = hi
        el[start : start + size, f * 128 : (f + 1) * 128] = lo

    def plane_faces(planes, edges):
        for side, x in ((0, 0), (1, CX - 1)):
            ph = planes[side, 0]
            h1, h2, h3, h4 = mobilities(ph, planes[side, 1], planes[side, 2])
            there, here = (h1, h2, h3 + h4), [q[f, x, 0:CY] for f in (1, 2, 3)]
            p = q[0, x, 0:CY]
            if side == 0:
                flow = side_flux(ph, there, p, here, txb[0])
            else:
                flow = side_flux(p, here, ph, there, txb[1])
            for f in range(3):
                base[f, x] = base[f, x] - flow[f] if side == 0 else base[f, x] + flow[f]
                if edges:
                    change = ns[f, x] * flow[f] if side == 0 else -ns[f, x] * flow[f]
                    put_edge(side * CY, CY, f, change)

    def row_faces(rows, rows_out, edges):
        row_edges = []
        for side, y in ((0, 0), (1, CY - 1)):
            ph = rows[side, 0]
            h1, h2, h3, h4 = mobilities(ph, rows[side, 1], rows[side, 2])
            own_side = 1 - side
            p = rows_out[own_side, 0]
            m1, m2, m3, m4 = mobilities(p, rows_out[own_side, 1], rows_out[own_side, 2])
            there, here = (h1, h2, h3 + h4), (m1, m2, m3 + m4)
            if side == 0:
                flow = side_flux(ph, there, p, here, tyb[0])
            else:
                flow = side_flux(p, here, ph, there, tyb[1])
            for f in range(3):
                change = -flow[f] if side == 0 else flow[f]
                for x in range(CX):
                    base[f, x, y : y + 1] = base[f, x, y : y + 1] + change[x : x + 1]
                if edges:
                    scale = jnp.concatenate([ns[f, x, y : y + 1] for x in range(CX)], axis=0)
                    row_edges.append((f, -scale * change))
        if edges:
            for f in range(3):
                put_edge(2 * CY, 16, f, jnp.concatenate([v for i, v in row_edges if i == f], axis=0))

    def transmissibility(x, c):
        k = st1[3, x]
        nxt = st1[3, jnp.minimum(x + 1, CX - 1)]
        tx[x] = harmonic(k, nxt) * jnp.where(x < CX - 1, 1.0, 0.0)
        ys = lax.broadcasted_iota(jnp.int32, (CY, NZ), 0)
        zs = lax.broadcasted_iota(jnp.int32, (CY, NZ), 1)
        ty[x] = jnp.where(ys == CY - 1, 0.0, harmonic(k, pltpu.roll(k, CY - 1, 0)))
        tz[x] = jnp.where(zs == NZ - 1, 0.0, 0.1 * harmonic(k, pltpu.roll(k, NZ - 1, 1)))
        return c

    def each_plane(body, first=0, last=CX):
        def step(x, c):
            body(x)
            return c
        lax.fori_loop(first, last, step, 0)

    def pack_wells_data():
        steps = lax.broadcasted_iota(jnp.int32, (8, 8), 0)
        spots = lax.broadcasted_iota(jnp.int32, (8, 8), 1)
        bottom = jnp.sum(jnp.where(steps == spots, bot_ref[...].reshape(1, 8), 0.0), axis=1, keepdims=True)
        parent = jnp.where(spots == 0, bottom, par_ref[...].astype(F32))
        steps = lax.broadcasted_iota(jnp.int32, (8, 128), 0)
        spots = lax.broadcasted_iota(jnp.int32, (8, 128), 1)
        repeat = jnp.where((spots & 7) == steps, 1.0, 0.0)
        both = exact_dot(jnp.concatenate([drop_ref[...], parent], axis=0), repeat)
        flat = jnp.where((spots >> 3) == steps, both[0:8], 0.0) + jnp.where((spots >> 3) - 8 == steps, both[8:16], 0.0)
        w0[...] = jnp.sum(flat, axis=0, keepdims=True)
        wr[gx, 0:1] = w0[...]

    def send_wells_data():
        for k in GX_ORDER:
            pltpu.make_async_remote_copy(
                w0, wr.at[gx, pl.ds(0, 1)], w_send, w_recv,
                device_id=(lax.rem(gx + k, NGX), gy), device_id_type=MESH,
            ).start()

    def place_wells_data():
        wait_bytes(wr.at[pl.ds(0, NGX - 1), pl.ds(0, 1)], w_recv)
        rows = jnp.concatenate([wr[i, 0:1] for i in range(NGX)], axis=0)
        parts = []
        for i in range(3):
            part = rows.astype(BF16)
            parts.append(part.astype(F32))
            rows = rows - parts[-1]
        spots = lax.broadcasted_iota(jnp.int32, (128, 2048), 1)
        wanted = ((spots >> 10) << 6) + ((spots & 7) << 3) + ((spots >> 7) & 7)
        repeat = jnp.where(lax.broadcasted_iota(jnp.int32, (128, 2048), 0) == wanted, 1.0, 0.0).astype(BF16)
        spread = jnp.dot(jnp.concatenate(parts, axis=0).astype(BF16), repeat, preferred_element_type=F32)
        spread = (spread[0:16] + spread[16:32]) + spread[32:48]
        spots = lax.broadcasted_iota(jnp.int32, (NGX, 2048), 1)
        mine = ((spots & 127) >> 3) == lax.broadcasted_iota(jnp.int32, (NGX, 2048), 0)
        spread = jnp.sum(jnp.where(mine, spread, 0.0), axis=0, keepdims=True)
        for seg in range(8):
            wd[seg : seg + 1, 0:128] = spread[:, seg * 128 : (seg + 1) * 128]
            wd[seg : seg + 1, 128:256] = spread[:, (seg + 8) * 128 : (seg + 9) * 128]

    def column_fields(x):
        here = pl.ds(pl.multiple_of(x * CY, CY), CY)
        fields = [st1[f, x] - ns[f, x] * base[f, x] for f in range(3)]
        fields += [ns[f, x] * q[f + 1, x, 0:CY] for f in range(3)]
        for f, field in enumerate(fields):
            hi, lo = split(field)
            dh[here, f * 128 : (f + 1) * 128] = hi
            dl[here, f * 128 : (f + 1) * 128] = lo

    place = jnp.where(
        lax.broadcasted_iota(jnp.int32, (8, 128), 0) + gx * 8 == lax.broadcasted_iota(jnp.int32, (8, 128), 1),
        1.0, 0.0,
    )
    flip = (((1,), (1,)), ((), ()))

    pack_wells_data()

    for i in range(3):
        loads[i].wait()
    for load in loads[5:]:
        load.start()
    each_plane(lambda x: prep(x, st1, True))
    loads[3].wait()
    seen = jnp.dot(g[...], mlh[...], preferred_element_type=F32) + jnp.dot(
        g[...], mll[...], preferred_element_type=F32
    )
    well_sums(0, seen[:, 0:128], seen[:, 128:256])
    loads[4].wait()
    pl.semaphore_wait(barrier, NGX - 1 + NGY - 1)
    k_copies = [
        pltpu.make_async_remote_copy(
            st1.at[3, x], hk.at[i], k_send.at[i], k_recv.at[i],
            device_id=(lax.rem(gx + step, NGX), gy), device_id_type=MESH,
        )
        for i, (x, step) in enumerate(((CX - 1, 1), (0, NGX - 1)))
    ]
    send_wells_data()
    halo_one = halo_copies(0, st1, hx1, hys1, hy1)
    early = plane_copies(0, 1, 2)
    late = plane_copies(1, 2, 4)
    for copy in k_copies + early:
        copy.start()
    send_one(0)

    pack_rows(st1, hys1, 4)
    for f in range(4):
        q[f, CX] = jnp.zeros((CY + 8, NZ), F32)
        for x in range(CX):
            q[f, x, CY : CY + 8] = jnp.zeros((8, NZ), F32)
    for f in range(3):
        fx[f] = jnp.zeros((CY, NZ), F32)
        fy[f, 0:8] = jnp.zeros((8, NZ), F32)
    each_row = lax.broadcasted_iota(jnp.int32, (128, PD), 0)
    for j in range(CX):
        s[j * 128 : (j + 1) * 128] = jnp.where(col == each_row + 128 * j, 1.0, 0.0).astype(BF16)
    here_t = ct[...]
    for j in range(3):
        same[:, j * 128 : (j + 1) * 128] = jnp.where(
            here_t == col[:, j * 128 : (j + 1) * 128], 1.0, 0.0
        ).astype(BF16)
    edge[:, 0:128] = g[:, 0:128]
    edge[:, 128:256] = g[:, COLS - 128 : COLS]
    spot = jnp.where(lanes < 8, lanes * 128, (lanes - 8) * 128 + 127)
    edge[:, 256:384] = jnp.where((here_t == spot) & (lanes < 16), 1.0, 0.0).astype(BF16)
    eh[256:384] = jnp.zeros((128, 384), BF16)
    el[256:384] = jnp.zeros((128, 384), BF16)
    hi, lo = split(cf[...])
    both = jnp.dot(s[...], jnp.concatenate([hi, lo], axis=1), preferred_element_type=F32)
    c0[...] = both[:, 0:128] + both[:, 128:256]
    lax.fori_loop(0, CX, transmissibility, 0)
    send_two(0)
    for copy in halo_one[2:] + late:
        copy.start()

    for i in range(5, 8):
        loads[i].wait()
    each_plane(lambda x: inner_faces(x, st1))
    each_plane(column_fields)
    place_wells_data()
    gq[...] = jnp.dot(g[...], dh[...], preferred_element_type=F32) + jnp.dot(
        g[...], dl[...], preferred_element_type=F32
    )
    send_three(0)

    for copy in k_copies + early + late + halo_one[2:]:
        copy.wait()
    for side, x, there in ((0, 0, gx > 0), (1, CX - 1, gx < NGX - 1)):
        txb[side] = harmonic(hk[side], st1[3, x]) * jnp.where(there, 1.0, 0.0)
    for side, there in ((0, gy > 0), (1, gy < NGY - 1)):
        tyb[side] = harmonic(hy1[side, 3], hys1[1 - side, 3]) * jnp.where(there, 1.0, 0.0)
    plane_faces(hx1, True)
    row_faces(hy1, hys1, True)
    gq[:, 0:384] = gq[:, 0:384] + (
        jnp.dot(edge[...], eh[...], preferred_element_type=F32)
        + jnp.dot(edge[...], el[...], preferred_element_type=F32)
    )
    answers(0)

    both = jnp.dot(same[...], vhl[...], preferred_element_type=F32)
    level = both[:, 0:128] + both[:, 128:256]
    p, sw, sg = (gq[:, f * 128 : (f + 1) * 128] + gq[:, (f + 3) * 128 : (f + 4) * 128] * level for f in range(3))
    m1, m2, m3, m4 = mobilities(p, sw, sg)
    well_sums(1, 0.8 * m1 + m2 + 0.15 * m3, total_mobility(sw, sg))
    send_one(1)
    spread_answers()

    def update(x):
        here = pl.ds(pl.multiple_of(x * CY, CY), CY)
        for f in range(3):
            first = base[f, x] - q[f + 1, x, 0:CY] * wl[here]
            st2[f, x] = st1[f, x] - ns[f, x] * first
        prep(x, st2, False)

    each_plane(update)
    pack_rows(st2, hys2, 3)
    halo_two = halo_copies(1, st2, hx2, hys2, hy2)
    for f in range(3):
        fx[f] = jnp.zeros((CY, NZ), F32)
    send_two(1)
    each_plane(lambda x: inner_faces(x, st2), 0, 5)
    for copy in halo_two:
        copy.start()
    each_plane(lambda x: inner_faces(x, st2), 5, CX)
    press = send_three(1)
    press_ref[...] = exact_dot(place, press, flip)
    for copy in halo_two:
        copy.wait()
    plane_faces(hx2, False)
    row_faces(hy2, hys2, False)
    answers(1)
    wait_bytes(wr.at[pl.ds(0, NGX - 1), pl.ds(0, 1)], w_send)
    for n in range(2):
        wait_bytes(r1.at[n], ph_send.at[n, 0])
        wait_bytes(in_parts[n], ph_send.at[n, 1])
        wait_bytes(r3.at[n, pl.ds(0, 56)], ph_send.at[n, 2])


def finish(base, q, s, vhl, press, out, press_out, held, sem):
    copies = [pltpu.make_async_copy(press, press_out, sem.at[CX])]
    copies[0].start()
    for start in range(0, CX, 2):
        both = jnp.dot(s[start * CY : (start + 2) * CY], vhl[...], preferred_element_type=F32)
        for x in range(start, start + 2):
            here = slice((x - start) * CY, (x - start + 1) * CY)
            wl = both[here, 0:128] + both[here, 128:256]
            for f in range(3):
                held[f, x] = base[f, x] - q[f + 1, x, 0:CY] * wl
            copies.append(pltpu.make_async_copy(held.at[:, x], out.at[:, x], sem.at[x]))
            copies[-1].start()
    for copy in copies:
        copy.wait()


def shards(
    pressure, water_sat, gas_sat, mass_old, pore_volume, permeability, newton_scale, conn_factor,
    perf_column, perf_owner, perf_well, perf_segment, seg_parent, seg_drop, bottom_press,
):
    vmem = pl.BlockSpec(memory_space=pltpu.VMEM)
    hbm = pl.BlockSpec(memory_space=pltpu.HBM)
    cells = (CX, CY, NZ)
    dma = pltpu.SemaphoreType.DMA
    scratch = [
        pltpu.VMEM((4,) + cells, F32),
        pltpu.VMEM((3,) + cells, F32),
        pltpu.VMEM((PD, NZ), F32),
        pltpu.VMEM(cells, F32),
        pltpu.VMEM((3,) + cells, F32),
        pltpu.VMEM((3,) + cells, F32),
        pltpu.VMEM((2, 3, CY, NZ), F32),
        pltpu.VMEM((2, 3, CY, NZ), F32),
        pltpu.VMEM((2, 4, CX, NZ), F32),
        pltpu.VMEM((2, 3, CX, NZ), F32),
        pltpu.VMEM((2, 4, CX, NZ), F32),
        pltpu.VMEM((2, 3, CX, NZ), F32),
        pltpu.VMEM((2, CY, NZ), F32),
        pltpu.VMEM(cells, F32),
        pltpu.VMEM(cells, F32),
        pltpu.VMEM(cells, F32),
        pltpu.VMEM((2, CY, NZ), F32),
        pltpu.VMEM((2, CX, NZ), F32),
        pltpu.VMEM((3, CY, NZ), F32),
        pltpu.VMEM((3, CY + 8, NZ), F32),
        pltpu.VMEM((COLS, NZ), F32),
        pltpu.VMEM((COLS, NZ), F32),
        pltpu.VMEM((PD, COLS), BF16),
        pltpu.VMEM((64, PD), BF16),
        pltpu.VMEM((PD, 128), BF16),
        pltpu.VMEM((PD, 128), F32),
        pltpu.VMEM((COLS, 256), BF16),
        pltpu.VMEM((COLS, 256), BF16),
        pltpu.VMEM((PD, PD), BF16),
        pltpu.VMEM((PD, 128), jnp.int32),
        pltpu.VMEM((PD, 384), BF16),
        pltpu.VMEM((COLS, 768), BF16),
        pltpu.VMEM((COLS, 768), BF16),
        pltpu.VMEM((PD, 768), F32),
        pltpu.VMEM((384, 384), BF16),
        pltpu.VMEM((384, 384), BF16),
        pltpu.VMEM((2, 64, 256), F32),
        pltpu.VMEM((2, NGY - 1, 8, 256), F32),
        pltpu.VMEM((8, 256), F32),
        pltpu.VMEM((NGX - 1, 8, 256), F32),
        pltpu.VMEM((8, 256), F32),
        pltpu.VMEM((NGX - 1, 8, 256), F32),
        pltpu.VMEM((2, 8, 256), F32),
        pltpu.VMEM((2, 64, 256), F32),
        pltpu.VMEM((1, 128), F32),
        pltpu.VMEM((NGX, 8, 128), F32),
        pltpu.VMEM((8, 256), F32),
        pltpu.VMEM((PD,), jnp.int32),
        pltpu.VMEM((1, PD), jnp.int32),
        pltpu.VMEM((PD,), jnp.int32),
        pltpu.VMEM((PD,), jnp.int32),
        pltpu.VMEM((8, 8), jnp.int32),
        pltpu.VMEM((8, 8), F32),
        pltpu.VMEM((8,), F32),
        dma((7,)), dma((8,)), dma((2, 4)), dma((2, 4)), dma((6,)), dma((6,)), dma, dma, dma((2, 3)), dma((2, 3)),
    ]
    fields = (
        pressure, water_sat, gas_sat, mass_old, pore_volume, permeability, newton_scale, conn_factor,
        perf_column, perf_owner.reshape(1, PD), perf_well, perf_segment, seg_parent, seg_drop, bottom_press,
    )
    results = pl.pallas_call(
        kernel,
        out_shape=(
            pltpu.VMEM((3,) + cells, F32),
            pltpu.VMEM((4, CX + 1, CY + 8, NZ), F32),
            pltpu.VMEM((COLS, PD), BF16),
            pltpu.VMEM((PD, 256), BF16),
            pltpu.VMEM((8, 8), F32),
        ),
        in_specs=[hbm] * 15,
        out_specs=(vmem,) * 5,
        scratch_shapes=scratch,
        compiler_params=pltpu.CompilerParams(
            collective_id=0, has_side_effects=True, vmem_limit_bytes=40 << 20
        ),
    )(*[pltpu.with_memory_space_constraint(v, pltpu.HBM) for v in fields])
    return pl.pallas_call(
        finish,
        out_shape=(jax.ShapeDtypeStruct((3,) + cells, F32), jax.ShapeDtypeStruct((8, 8), F32)),
        in_specs=[vmem] * 5,
        out_specs=(hbm, hbm),
        scratch_shapes=[pltpu.VMEM((3,) + cells, F32), dma((CX + 1,))],
        compiler_params=pltpu.CompilerParams(vmem_limit_bytes=6 << 20),
    )(*[pltpu.with_memory_space_constraint(v, pltpu.VMEM) for v in results])


def solution(mesh):
    cell = P("gx", "gy", None)
    triple = P(None, "gx", "gy", None)
    flat = P(("gx", "gy"))
    rows = P(("gx", "gy"), None)
    return jax.shard_map(
        shards,
        mesh=mesh,
        in_specs=(
            cell, cell, cell, triple, cell, cell, triple,
            rows, flat, rows, flat, flat, rows, rows, flat,
        ),
        out_specs=(triple, rows),
        check_vma=False,
    )
```
